256 devices in a mesh: row: 32 (over x_lo, z, core), col: 4 (over y), rep: 2 (over x_hi).
Axes of the slice: x: 4 (x_hi: 2, x_lo: 2; x = x_hi * 2 + x_lo), y: 4, z: 8, core: 2. Of those that a mesh axis runs over, the one named last changes fastest.
Arguments:
- queries: bfloat16 [131072, 768], P(('rep', 'row', 'col')), parts along dimension 0, may hold values from -16 to 16
- passages: bfloat16 [98304, 768], P(('rep', 'row', 'col')), parts along dimension 0, may hold values from -16 to 16
- positive: int32 [131072], P(('rep', 'row', 'col')), parts along dimension 0, may hold values from 0 to 383
- block_mask: int32 [131072, 15], P(('rep', 'row', 'col')), parts along dimension 0, may hold values from 0 to 1
- roster: int32 [131072, 3], P(('rep', 'row', 'col')), parts along dimension 0, may hold values from 0 to 2
Outputs:
- loss: float32 [2], P('rep'), parts along dimension 0
- grad_queries: float32 [131072, 768], P(('rep', 'row', 'col')), parts along dimension 0
- grad_passages: float32 [98304, 768], P(('rep', 'row', 'col')), parts along dimension 0
The draws below stay inside these ranges and needn't reach their ends.
There are 2 independent parts, one for each index of `rep`. The reference program is written for one: setup_inputs(seed, part) draws one part's arguments, and reference() takes and returns one part's arrays. A program takes and returns all parts, laid end to end along the dimension named above; each array names one. Nothing has to cross between parts.
All inputs are finite; a program needn't handle non-finite values.
Results may differ from the reference program's by a relative error of at most 0.002.
Values may be sent and summed in bfloat16 or wider, within the bound.
A program may use at most 128 MiB of HBM per device.

```python
import math
import jax
import jax.numpy as jnp
from jax import lax

D = 768
Q_DEV = 512
P_DEV = 384
BLK = 128
PB = 3
REACH = 2
NB = 15
QN = 65536
PN = 49152
N_ROW = 32
N_COL = 4


def positive_rows(key):
    return jax.random.randint(jax.random.fold_in(key, 7), (QN,), 0, P_DEV, dtype=jnp.int32)


def embedding_pair(key):
    keys = [jax.random.fold_in(key, 100 + number) for number in range(8)]
    base_q = jnp.clip(jax.random.normal(keys[0], (QN, D), jnp.float32), -4.0, 4.0)
    base_p = jnp.clip(jax.random.normal(keys[1], (PN, D), jnp.float32), -4.0, 4.0)
    scale_q = jnp.exp(jax.random.uniform(keys[2], (QN, 1), jnp.float32, math.log(0.3), math.log(3.0)))
    scale_p = jnp.exp(jax.random.uniform(keys[3], (PN, 1), jnp.float32, math.log(0.3), math.log(3.0)))
    queries = scale_q * base_q
    passages = scale_p * base_p
    return (queries, passages)


def draw_queries(key, part):
    return embedding_pair(key)[0].astype(jnp.bfloat16)


def draw_passages(key, part):
    return embedding_pair(key)[1].astype(jnp.bfloat16)


def draw_positive(key, part):
    return positive_rows(key)


def draw_block_mask(key, part):
    cells = QN // Q_DEV
    level = jax.random.randint(jax.random.fold_in(key, 21), (cells, 1, 1), 1, 5, dtype=jnp.int32)
    alive = jax.random.randint(jax.random.fold_in(key, 22), (cells, 1, NB), 0, 4, dtype=jnp.int32) < level
    coins = jax.random.randint(jax.random.fold_in(key, 23), (cells, Q_DEV, NB), 0, 2, dtype=jnp.int32)
    return (coins * alive.astype(jnp.int32)).reshape(QN, NB)


def place_ends(array, own_key, smallest, top_value):
    longest = array.shape.index(max(array.shape))
    spots = []
    for shift in (0, 1):
        where = [jax.random.randint(jax.random.fold_in(own_key, axis), (), 0, length) for axis, length in enumerate(array.shape)]
        where[longest] = (where[longest] + shift) % array.shape[longest]
        spots.append(tuple(where))
    return array.at[spots[0]].set(smallest).at[spots[1]].set(top_value)


def setup_inputs(seed: int = 0, part: int = 0) -> dict:
    streams_of = jax.random.split(jax.random.key(seed), 6)
    part_keys = jax.random.split(jax.random.fold_in(streams_of[5], part), 6)
    queries = draw_queries(jax.random.fold_in(jax.random.fold_in(streams_of[5], part), 71), part)
    passages = draw_passages(jax.random.fold_in(jax.random.fold_in(streams_of[5], part), 71), part)
    positive = draw_positive(jax.random.fold_in(jax.random.fold_in(streams_of[5], part), 71), part)
    block_mask = draw_block_mask(jax.random.fold_in(jax.random.fold_in(streams_of[5], part), 71), part)
    roster = place_ends(jax.random.randint(part_keys[4], (QN, N_COL - 1), 0, PB), jax.random.fold_in(part_keys[4], 1), 0, PB - 1).astype(jnp.int32)
    return {"queries": queries, "passages": passages, "positive": positive, "block_mask": block_mask, "roster": roster}


def visited_cells(cell_at):
    row_at = cell_at // N_COL
    col_at = cell_at % N_COL
    listed = [cell_at]
    for offset in list(range(-REACH, 0)) + list(range(1, REACH + 1)):
        listed.append(((row_at + offset) % N_ROW) * N_COL + col_at)
    for stride in range(1, N_COL):
        listed.append(row_at * N_COL + (col_at - stride) % N_COL)
    return listed


def reference(queries, passages, positive, block_mask, roster):
    scale = D ** -0.5
    block_ids = jnp.arange(P_DEV, dtype=jnp.int32) // BLK
    group_count = N_COL + 2 * REACH
    column_all = jnp.arange(group_count * P_DEV, dtype=jnp.int32)

    def one_cell(carried, cell_at):
        grad_rows, loss_sum = carried
        first = (cell_at * Q_DEV).astype(jnp.int32)
        query_rows = lax.dynamic_slice_in_dim(queries, first, Q_DEV, 0)
        targets = lax.dynamic_slice_in_dim(positive, first, Q_DEV, 0)
        masks_here = lax.dynamic_slice_in_dim(block_mask, first, Q_DEV, 0)
        plans_here = lax.dynamic_slice_in_dim(roster, first, Q_DEV, 0)
        visited = visited_cells(cell_at)
        cell_rows = jnp.concatenate([lax.dynamic_slice_in_dim(passages, (other * P_DEV).astype(jnp.int32), P_DEV, 0) for other in visited], axis=0)
        parts_seen = [(jnp.repeat(masks_here[:, 0:PB], BLK, axis=1) == 1) | (block_ids[None, :] == (targets // BLK)[:, None])]
        for group_at in range(1, 2 * REACH + 1):
            parts_seen.append(jnp.repeat(masks_here[:, group_at * PB:(group_at + 1) * PB], BLK, axis=1) == 1)
        for stride in range(1, N_COL):
            parts_seen.append(block_ids[None, :] == plans_here[:, stride - 1:stride])
        visible = jnp.concatenate(parts_seen, axis=1)
        scores = jnp.dot(query_rows, cell_rows.T, preferred_element_type=jnp.float32) * scale
        highest = jnp.max(jnp.where(visible, scores, -jnp.inf), axis=1)
        summed = jnp.sum(jnp.where(visible, jnp.exp(scores - highest[:, None]), 0.0), axis=1)
        log_total = highest + jnp.log(summed)
        target_mask = column_all[None, :] == targets[:, None]
        positive_score = jnp.sum(jnp.where(target_mask, scores, 0.0), axis=1)
        weights = jnp.where(visible, jnp.exp(scores - log_total[:, None]), 0.0) - target_mask.astype(jnp.float32)
        weights = weights.astype(jnp.bfloat16)
        toward = jnp.dot(weights, cell_rows, preferred_element_type=jnp.float32) * scale
        pieces = lax.dot_general(weights, query_rows, (((0,), (0,)), ((), ())), preferred_element_type=jnp.float32) * scale
        for group_at, other in enumerate(visited):
            start = (other * P_DEV).astype(jnp.int32)
            former = lax.dynamic_slice_in_dim(grad_rows, start, P_DEV, 0)
            grad_rows = lax.dynamic_update_slice_in_dim(grad_rows, former + pieces[group_at * P_DEV:(group_at + 1) * P_DEV], start, 0)
        loss_sum = loss_sum + jnp.sum(log_total - positive_score)
        return (grad_rows, loss_sum), toward

    initial = (jnp.zeros((PN, D), jnp.float32), jnp.zeros((), jnp.float32))
    (grad_passages, loss_sum), towards = lax.scan(one_cell, initial, jnp.arange(N_ROW * N_COL, dtype=jnp.int32))
    return (loss_sum / QN).reshape(1), towards.reshape(QN, D), grad_passages
```

```python
import functools

import jax
import jax.numpy as jnp
from jax import lax
from jax.experimental import pallas as pl
from jax.experimental.pallas import tpu as pltpu
from jax.sharding import PartitionSpec as P

MESH = pl.DeviceIdType.MESH
BLK = 128
LOWEST = -1e30
F32, BF16, I32 = jnp.float32, jnp.bfloat16, jnp.int32

OWN, SIB, FRONT, BACK, FAR, Y1, Y2, Y3 = range(8)
SEEN_AS = {SIB: SIB, FRONT: BACK, BACK: FRONT, FAR: FAR, Y1: Y3, Y2: Y2, Y3: Y1}
LOSS_BITS = (1, 16, 2, 4, 8)


def nt(a, b):
    return lax.dot_general(a, b, (((1,), (1,)), ((), ())), preferred_element_type=F32)


def tn(a, b):
    return lax.dot_general(a, b, (((0,), (0,)), ((), ())), preferred_element_type=F32)


def kernel(
    n_row, n_col,
    q_hbm, p_hbm, pos_hbm, bm_hbm, ro_hbm,
    loss_ref, gq_ref, gp_ref,
    q, pall, qr, pos, bm, ro, vis, ebuf, wbuf, mrow, run_m, run_l, lt, psc, meta_out, meta_in, lout, lin,
    loc_s, p_ss, p_rs, q_ss, q_rs, m_ss, m_rs, l_ss, l_rs,
):
    nq, width = q.shape
    np_ = pall.shape[1]
    blocks = np_ // BLK
    scale = width ** (-0.5)
    hq, hp = nq // 2, np_ // 2
    r, c = lax.axis_index("row"), lax.axis_index("col")
    odd = lax.rem(r, 2)
    s = 1 - 2 * odd

    def at_row(o):
        return {"row": lax.rem(r + o + n_row, n_row), "col": c}

    def at_col(o):
        return {"row": r, "col": lax.rem(c + o + n_col, n_col)}

    where = {
        SIB: at_row(s), FRONT: at_row(2 * s), BACK: at_row(-2 * s), FAR: at_row(-s),
        Y1: at_col(-1), Y2: at_col(-2), Y3: at_col(1),
    }
    partner = {
        b: {"row": r + b - 2 * b * lax.rem(lax.div(r, b), 2), "col": c} for b in LOSS_BITS
    }

    barrier = pltpu.get_barrier_semaphore()
    greeted = list(where.values()) + [partner[b] for b in (4, 8, 16)]
    for d in greeted:
        pl.semaphore_signal(barrier, inc=1, device_id=d, device_id_type=MESH)

    loads = [
        pltpu.make_async_copy(src, dst, loc_s.at[i])
        for i, (src, dst) in enumerate(
            ((q_hbm, q), (p_hbm, pall.at[OWN]), (bm_hbm, bm), (ro_hbm, ro), (pos_hbm, pos))
        )
    ]
    for cp in loads:
        cp.start()
    pl.semaphore_wait(barrier, len(greeted))

    class Sender:
        def __init__(self, ss, rs, land):
            self.ss, self.rs, self.land, self.n, self.sent = ss, rs, land, 0, []

        def __call__(self, src, slot, to, first, rows, mark):
            cp = pltpu.make_async_remote_copy(
                src_ref=src.at[pl.ds(first, rows)],
                dst_ref=self.land(slot).at[pl.ds(first, rows)],
                send_sem=self.ss.at[self.n],
                recv_sem=self.rs.at[slot, mark],
                device_id=where[to],
                device_id_type=MESH,
            )
            self.n += 1
            self.sent.append(cp)
            cp.start()
            return cp

    send_p = Sender(p_ss, p_rs, lambda k: pall.at[k])
    send_q = Sender(q_ss, q_rs, lambda k: qr.at[k - 1])

    pa0 = send_p(p_hbm, Y1, Y3, 0, hp, 0)
    pb1 = send_p(p_hbm, Y3, Y1, hp, hp, 1)
    p_front = send_p(p_hbm, BACK, FRONT, 0, np_, 0)
    p_back = send_p(p_hbm, FRONT, BACK, 0, np_, 0)
    p_sib = send_p(p_hbm, SIB, SIB, 0, np_, 0)
    pa1 = send_p(p_hbm, Y1, Y3, hp, hp, 1)
    pb0 = send_p(p_hbm, Y3, Y1, 0, hp, 0)
    q_sib = send_q(q_hbm, SIB, SIB, 0, nq, 0)
    q_front = [send_q(q_hbm, BACK, FRONT, 0, hq, 0)]
    q_back = [send_q(q_hbm, FRONT, BACK, 0, hq, 0)]

    for cp in loads:
        cp.wait()
    row_i = lax.broadcasted_iota(I32, (64, 1), 0)
    slot_i, block_i = lax.shift_right_logical(row_i, 3), lax.bitwise_and(row_i, 7)
    up = jnp.where(odd == 0, jnp.int32(1), jnp.int32(0))
    group = jnp.where(
        slot_i == SIB, 2 + up,
        jnp.where(slot_i == FRONT, 1 + 3 * up, jnp.where(slot_i == BACK, 4 - 3 * up, jnp.where(slot_i == FAR, 3 - up, 0))),
    )
    nb = bm.shape[1]
    wanted = jnp.where((slot_i <= FAR) & (block_i < blocks), group * blocks + block_i, -1)
    pick = jnp.where(lax.broadcasted_iota(I32, (64, nb), 1) == wanted, 1.0, 0.0).astype(BF16)
    seen = nt(pick, bm[...].astype(F32).astype(BF16))
    nr = ro.shape[1]
    pick_r = jnp.where(lax.broadcasted_iota(I32, (64, nr), 1) == slot_i - Y1, 1.0, 0.0).astype(BF16)
    listed = nt(pick_r, ro[...].astype(F32).astype(BF16))
    in_roster = jnp.where(jnp.abs(listed - block_i.astype(F32)) < 0.5, 1.0, 0.0)
    seen = jnp.where(slot_i >= Y1, in_roster, seen)
    pos_row = pos[...]
    own_block = jnp.where((slot_i == OWN) & (lax.shift_right_logical(pos_row, 7) == block_i), 1.0, 0.0)
    seen = jnp.maximum(seen, own_block)
    for k in range(8):
        vis[k] = seen[8 * k : 8 * k + 8]

    run_m[...] = jnp.full(run_m.shape, LOWEST, F32)
    run_l[...] = jnp.zeros(run_l.shape, F32)

    def forward(k):
        @pl.loop(0, 2)
        def _(h):
            cols = pl.ds(pl.multiple_of(h * hq, hq), hq)
            sc = nt(pall[k], q[cols, :]) * scale
            v = vis[k, :, cols]
            m_old = run_m[0:1, cols]
            m_new = m_old
            for b in range(blocks):
                top = jnp.max(sc[b * BLK : (b + 1) * BLK], axis=0, keepdims=True)
                m_new = jnp.maximum(m_new, jnp.where(v[b : b + 1] > 0.5, top, LOWEST))
            total = run_l[0:1, cols] * jnp.exp(m_old - m_new)
            for b in range(blocks):
                bias = jnp.where(v[b : b + 1] > 0.5, -m_new, LOWEST)
                e = jnp.exp(sc[b * BLK : (b + 1) * BLK] + bias)
                total = total + jnp.sum(e, axis=0, keepdims=True)
                ebuf[k, b * BLK : (b + 1) * BLK, cols] = e
            if k == OWN:
                target = lax.broadcasted_iota(I32, (np_, hq), 0) == pos[0:1, cols]
                psc[0:1, cols] = jnp.sum(jnp.where(target, sc, 0.0), axis=0, keepdims=True)
            run_m[0:1, cols] = m_new
            run_l[0:1, cols] = total
            mrow[k, 0:1, cols] = m_new

    forward(OWN)
    p_sib.wait_recv()
    forward(SIB)
    pa0.wait_recv()
    ra = send_p(pall.at[Y1], Y2, Y3, 0, hp, 0)
    pb1.wait_recv()
    rb = send_p(pall.at[Y3], Y2, Y1, hp, hp, 1)
    p_back.wait_recv()
    p_far = send_p(pall.at[FRONT], FAR, SIB, 0, np_, 0)
    p_front.wait_recv()
    pa1.wait_recv()
    pb0.wait_recv()
    qa = [send_q(q_hbm, Y1, Y3, 0, hq, 0)]
    qb = [send_q(q_hbm, Y3, Y1, hq, hq, 1)]
    forward(FRONT)
    forward(BACK)
    forward(Y1)
    forward(Y3)
    p_far.wait_recv()
    forward(FAR)
    ra.wait_recv()
    rb.wait_recv()
    forward(Y2)

    lt[0:1] = run_m[0:1] + jnp.log(run_l[0:1])
    own_loss = jnp.sum(lt[0:1] - psc[0:1], axis=1, keepdims=True)
    metas = {}
    for k in (Y1, Y3, FRONT, BACK, SIB, FAR, Y2):
        rows = jnp.where(vis[k] > 0.5, -lt[0:1], LOWEST)
        last = lax.broadcasted_iota(I32, rows.shape, 0) == 7
        meta_out[k] = jnp.where(last, own_loss, rows)
        seen_as = SEEN_AS[k]
        cp = pltpu.make_async_remote_copy(
            src_ref=meta_out.at[k], dst_ref=meta_in.at[seen_as],
            send_sem=m_ss.at[k], recv_sem=m_rs.at[seen_as],
            device_id=where[k], device_id_type=MESH,
        )
        cp.start()
        metas[seen_as] = cp
    q_front.append(send_q(q_hbm, BACK, FRONT, hq, hq, 1))
    q_back.append(send_q(q_hbm, FRONT, BACK, hq, hq, 1))
    qa.append(send_q(q_hbm, Y1, Y3, hq, hq, 1))
    qb.append(send_q(q_hbm, Y3, Y1, 0, hq, 0))
    q_back[0].wait_recv()
    q_far = [send_q(qr.at[FRONT - 1], FAR, SIB, 0, hq, 0)]

    for k in range(8):
        @pl.loop(0, 2)
        def _(h):
            cols = pl.ds(pl.multiple_of(h * hq, hq), hq)
            factor = jnp.exp(mrow[k, 0:1, cols] - lt[0:1, cols])
            w = ebuf[k, :, cols] * factor
            if k == OWN:
                target = lax.broadcasted_iota(I32, (np_, hq), 0) == pos[0:1, cols]
                w = w - jnp.where(target, 1.0, 0.0)
            wbuf[k * np_ : (k + 1) * np_, cols] = w.astype(BF16)

    gp_ref[...] = jnp.dot(wbuf[0:np_, :], q[...], preferred_element_type=F32) * scale

    @pl.loop(0, 2)
    def _(h):
        cols = pl.ds(pl.multiple_of(h * hq, hq), hq)
        total = tn(wbuf[0:np_, cols], pall[0])
        for k in range(1, 8):
            total = total + tn(wbuf[k * np_ : (k + 1) * np_, cols], pall[k])
        gq_ref[cols, :] = total * scale

    def backward(k, first, rows):
        span = pl.ds(first, rows)
        sc = nt(pall[OWN], qr[k - 1, span, :]) * scale
        parts = []
        for b in range(blocks):
            parts.append(jnp.exp(sc[b * BLK : (b + 1) * BLK] + meta_in[k, b : b + 1, span]).astype(BF16))
        w = jnp.concatenate(parts, axis=0)
        gp_ref[...] += jnp.dot(w, qr[k - 1, span, :], preferred_element_type=F32) * scale

    loss_steps = []

    def loss_send(i, value):
        lout[i] = value
        cp = pltpu.make_async_remote_copy(
            src_ref=lout.at[i], dst_ref=lin.at[i], send_sem=l_ss.at[i], recv_sem=l_rs.at[i],
            device_id=partner[LOSS_BITS[i]], device_id_type=MESH,
        )
        cp.start()
        loss_steps.append(cp)

    def loss_next(i):
        loss_steps[i].wait_recv()
        value = lout[i] + lin[i]
        if i + 1 < len(LOSS_BITS):
            loss_send(i + 1, value)
        else:
            loss_ref[...] = value * (1.0 / (nq * n_row * n_col))

    metas[SIB].wait_recv()
    q_sib.wait_recv()
    backward(SIB, 0, hq)
    backward(SIB, hq, hq)
    metas[FRONT].wait_recv()
    backward(FRONT, 0, hq)
    metas[BACK].wait_recv()
    q_front[0].wait_recv()
    backward(BACK, 0, hq)
    metas[FAR].wait_recv()
    q_far[0].wait_recv()
    backward(FAR, 0, hq)

    qa[0].wait_recv()
    ra2 = [send_q(qr.at[Y1 - 1], Y2, Y3, i * hq // 2, hq // 2, i) for i in range(2)]
    qb[0].wait_recv()
    rb2 = [send_q(qr.at[Y3 - 1], Y2, Y1, hq + i * hq // 2, hq // 2, 2 + i) for i in range(2)]
    metas[Y1].wait_recv()
    metas[Y3].wait_recv()
    metas[Y2].wait_recv()
    spread = lax.broadcasted_iota(I32, (8, 128), 0) >= 0
    loss_at = lambda k: meta_in[k, 7:8, 0:128]
    near = loss_at(Y1) + loss_at(Y3)
    mine = meta_out[Y1, 7:8, 0:128] + loss_at(Y2)
    loss_send(0, jnp.where(spread, near + mine, 0.0))
    backward(Y1, 0, hq)
    backward(Y3, hq, hq)
    loss_next(0)
    q_back[1].wait_recv()
    q_far.append(send_q(qr.at[FRONT - 1], FAR, SIB, hq, hq, 1))
    backward(FRONT, hq, hq)
    q_front[1].wait_recv()
    backward(BACK, hq, hq)
    loss_next(1)
    q_far[1].wait_recv()
    backward(FAR, hq, hq)
    loss_next(2)
    qa[1].wait_recv()
    backward(Y1, hq, hq)
    loss_next(3)
    qb[1].wait_recv()
    backward(Y3, 0, hq)
    loss_next(4)
    for i in range(2):
        ra2[i].wait_recv()
        backward(Y2, i * hq // 2, hq // 2)
        rb2[i].wait_recv()
        backward(Y2, hq + i * hq // 2, hq // 2)

    for cp in send_p.sent + send_q.sent + list(metas.values()) + loss_steps:
        cp.wait_send()


def local(n_row, n_col, queries, passages, positive, block_mask, roster):
    nq, width = queries.shape
    np_ = passages.shape[0]
    nb, nr = block_mask.shape[1], roster.shape[1]
    anywhere = pl.BlockSpec(memory_space=pl.ANY)
    inside = pl.BlockSpec(memory_space=pltpu.VMEM)
    dma = pltpu.SemaphoreType.DMA
    loss, gq, gp = pl.pallas_call(
        functools.partial(kernel, n_row, n_col),
        out_shape=(
            jax.ShapeDtypeStruct((8, 128), F32),
            jax.ShapeDtypeStruct((nq, width), F32),
            jax.ShapeDtypeStruct((np_, width), F32),
        ),
        in_specs=[anywhere] * 5,
        out_specs=(inside,) * 3,
        scratch_shapes=[
            pltpu.VMEM((nq, width), BF16),
            pltpu.VMEM((8, np_, width), BF16),
            pltpu.VMEM((7, nq, width), BF16),
            pltpu.VMEM((1, nq), I32),
            pltpu.VMEM((nq, nb), I32),
            pltpu.VMEM((nq, nr), I32),
            pltpu.VMEM((8, 8, nq), F32),
            pltpu.VMEM((8, np_, nq), F32),
            pltpu.VMEM((8 * np_, nq), BF16),
            pltpu.VMEM((8, 8, nq), F32),
            pltpu.VMEM((8, nq), F32),
            pltpu.VMEM((8, nq), F32),
            pltpu.VMEM((8, nq), F32),
            pltpu.VMEM((8, nq), F32),
            pltpu.VMEM((8, 8, nq), F32),
            pltpu.VMEM((8, 8, nq), F32),
            pltpu.VMEM((5, 8, 128), F32),
            pltpu.VMEM((5, 8, 128), F32),
            dma((5,)),
            dma((10,)),
            dma((8, 2)),
            dma((16,)),
            dma((8, 4)),
            dma((8,)),
            dma((8,)),
            dma((5,)),
            dma((5,)),
        ],
        compiler_params=pltpu.CompilerParams(
            collective_id=0, has_side_effects=True, vmem_limit_bytes=48 * 2**20
        ),
        cost_estimate=pl.CostEstimate(flops=10**10, bytes_accessed=10**7, transcendentals=4 * 10**6),
    )(queries, passages, positive.reshape(1, nq), block_mask, roster)
    return loss[0, 0:1], gq, gp


def solution(mesh):
    whole = P(("rep", "row", "col"), None)
    return jax.shard_map(
        functools.partial(local, mesh.shape["row"], mesh.shape["col"]),
        mesh=mesh,
        in_specs=(whole, whole, P(("rep", "row", "col")), whole, whole),
        out_specs=(P("rep"), whole, whole),
        check_vma=False,
    )
```

```python
import functools

import jax
import jax.numpy as jnp
from jax import lax
from jax.experimental import pallas as pl
from jax.experimental.pallas import tpu as pltpu
from jax.sharding import PartitionSpec as P

MESH = pl.DeviceIdType.MESH
BLK = 128
LOWEST = -1e30
F32, BF16, I32 = jnp.float32, jnp.bfloat16, jnp.int32

OWN, SIB, FRONT, BACK, FAR, Y1, Y2, Y3 = range(8)
SEEN_AS = {SIB: SIB, FRONT: BACK, BACK: FRONT, FAR: FAR, Y1: Y3, Y2: Y2, Y3: Y1}
LOSS_BITS = (1, 16, 2, 4, 8)


def nt(a, b):
    return lax.dot_general(a, b, (((1,), (1,)), ((), ())), preferred_element_type=F32)


def tn(a, b):
    return lax.dot_general(a, b, (((0,), (0,)), ((), ())), preferred_element_type=F32)


def kernel(
    n_row, n_col,
    q_hbm, p_hbm, pos_hbm, bm_hbm, ro_hbm,
    loss_ref, gq_ref, gp_ref,
    q, pall, qr, pos, bm, ro, vis, ebuf, wbuf, mrow, run_m, run_l, lt, psc, meta_out, meta_in, lout, lin,
    loc_s, p_ss, p_rs, q_ss, q_rs, m_ss, m_rs, l_ss, l_rs,
):
    nq, width = q.shape
    np_ = pall.shape[1]
    blocks = np_ // BLK
    scale = width ** (-0.5)
    hq, hp = nq // 2, np_ // 2
    r, c = lax.axis_index("row"), lax.axis_index("col")
    odd = lax.rem(r, 2)
    s = 1 - 2 * odd

    def at_row(o):
        return {"row": lax.rem(r + o + n_row, n_row), "col": c}

    def at_col(o):
        return {"row": r, "col": lax.rem(c + o + n_col, n_col)}

    where = {
        SIB: at_row(s), FRONT: at_row(2 * s), BACK: at_row(-2 * s), FAR: at_row(-s),
        Y1: at_col(-1), Y2: at_col(-2), Y3: at_col(1),
    }
    partner = {
        b: {"row": r + b - 2 * b * lax.rem(lax.div(r, b), 2), "col": c} for b in LOSS_BITS
    }

    barrier = pltpu.get_barrier_semaphore()
    greeted = list(where.values()) + [partner[b] for b in (4, 8, 16)]
    for d in greeted:
        pl.semaphore_signal(barrier, inc=1, device_id=d, device_id_type=MESH)

    loads = [
        pltpu.make_async_copy(src, dst, loc_s.at[i])
        for i, (src, dst) in enumerate(
            ((q_hbm, q), (p_hbm, pall.at[OWN]), (bm_hbm, bm), (ro_hbm, ro), (pos_hbm, pos))
        )
    ]
    for cp in loads:
        cp.start()
    pl.semaphore_wait(barrier, len(greeted))

    class Sender:
        def __init__(self, ss, rs, land):
            self.ss, self.rs, self.land, self.n, self.sent = ss, rs, land, 0, []

        def __call__(self, src, slot, to, first, rows, mark):
            cp = pltpu.make_async_remote_copy(
                src_ref=src.at[pl.ds(first, rows)],
                dst_ref=self.land(slot).at[pl.ds(first, rows)],
                send_sem=self.ss.at[self.n],
                recv_sem=self.rs.at[slot, mark],
                device_id=where[to],
                device_id_type=MESH,
            )
            self.n += 1
            self.sent.append(cp)
            cp.start()
            return cp

    send_p = Sender(p_ss, p_rs, lambda k: pall.at[k])
    send_q = Sender(q_ss, q_rs, lambda k: qr.at[k - 1])

    pa0 = send_p(p_hbm, Y1, Y3, 0, hp, 0)
    pb1 = send_p(p_hbm, Y3, Y1, hp, hp, 1)
    p_front = send_p(p_hbm, BACK, FRONT, 0, np_, 0)
    p_back = send_p(p_hbm, FRONT, BACK, 0, np_, 0)
    p_sib = send_p(p_hbm, SIB, SIB, 0, np_, 0)
    pa1 = send_p(p_hbm, Y1, Y3, hp, hp, 1)
    pb0 = send_p(p_hbm, Y3, Y1, 0, hp, 0)
    q_sib = send_q(q_hbm, SIB, SIB, 0, nq, 0)
    q_front = [send_q(q_hbm, BACK, FRONT, 0, hq, 0)]
    q_back = [send_q(q_hbm, FRONT, BACK, 0, hq, 0)]

    for cp in loads:
        cp.wait()
    row_i = lax.broadcasted_iota(I32, (64, 1), 0)
    slot_i, block_i = lax.shift_right_logical(row_i, 3), lax.bitwise_and(row_i, 7)
    up = jnp.where(odd == 0, jnp.int32(1), jnp.int32(0))
    group = jnp.where(
        slot_i == SIB, 2 + up,
        jnp.where(slot_i == FRONT, 1 + 3 * up, jnp.where(slot_i == BACK, 4 - 3 * up, jnp.where(slot_i == FAR, 3 - up, 0))),
    )
    nb = bm.shape[0]
    wanted = jnp.where((slot_i <= FAR) & (block_i < blocks), group * blocks + block_i, -1)
    pick = jnp.where(lax.broadcasted_iota(I32, (64, nb), 1) == wanted, 1.0, 0.0).astype(BF16)
    seen = jnp.dot(pick, bm[...].astype(F32).astype(BF16), preferred_element_type=F32)
    nr = ro.shape[0]
    pick_r = jnp.where(lax.broadcasted_iota(I32, (64, nr), 1) == slot_i - Y1, 1.0, 0.0).astype(BF16)
    listed = jnp.dot(pick_r, ro[...].astype(F32).astype(BF16), preferred_element_type=F32)
    in_roster = jnp.where(jnp.abs(listed - block_i.astype(F32)) < 0.5, 1.0, 0.0)
    seen = jnp.where(slot_i >= Y1, in_roster, seen)
    pos_row = pos[...]
    own_block = jnp.where((slot_i == OWN) & (lax.shift_right_logical(pos_row, 7) == block_i), 1.0, 0.0)
    seen = jnp.maximum(seen, own_block)
    for k in range(8):
        vis[k] = seen[8 * k : 8 * k + 8]

    run_m[...] = jnp.full(run_m.shape, LOWEST, F32)
    run_l[...] = jnp.zeros(run_l.shape, F32)

    def forward(k):
        @pl.loop(0, 2)
        def _(h):
            cols = pl.ds(pl.multiple_of(h * hq, hq), hq)
            sc = nt(pall[k], q[cols, :]) * scale
            v = vis[k, :, cols]
            m_old = run_m[0:1, cols]
            m_new = m_old
            for b in range(blocks):
                top = jnp.max(sc[b * BLK : (b + 1) * BLK], axis=0, keepdims=True)
                m_new = jnp.maximum(m_new, jnp.where(v[b : b + 1] > 0.5, top, LOWEST))
            total = run_l[0:1, cols] * jnp.exp(m_old - m_new)
            for b in range(blocks):
                bias = jnp.where(v[b : b + 1] > 0.5, -m_new, LOWEST)
                e = jnp.exp(sc[b * BLK : (b + 1) * BLK] + bias)
                total = total + jnp.sum(e, axis=0, keepdims=True)
                ebuf[k, b * BLK : (b + 1) * BLK, cols] = e
            if k == OWN:
                target = lax.broadcasted_iota(I32, (np_, hq), 0) == pos[0:1, cols]
                psc[0:1, cols] = jnp.sum(jnp.where(target, sc, 0.0), axis=0, keepdims=True)
            run_m[0:1, cols] = m_new
            run_l[0:1, cols] = total
            mrow[k, 0:1, cols] = m_new

    forward(OWN)
    p_sib.wait_recv()
    forward(SIB)
    pa0.wait_recv()
    ra = send_p(pall.at[Y1], Y2, Y3, 0, hp, 0)
    pb1.wait_recv()
    rb = send_p(pall.at[Y3], Y2, Y1, hp, hp, 1)
    p_back.wait_recv()
    p_far = send_p(pall.at[FRONT], FAR, SIB, 0, np_, 0)
    p_front.wait_recv()
    pa1.wait_recv()
    pb0.wait_recv()
    qa = [send_q(q_hbm, Y1, Y3, 0, hq, 0)]
    qb = [send_q(q_hbm, Y3, Y1, hq, hq, 1)]
    forward(FRONT)
    forward(BACK)
    forward(Y1)
    forward(Y3)
    p_far.wait_recv()
    forward(FAR)
    ra.wait_recv()
    rb.wait_recv()
    forward(Y2)

    lt[0:1] = run_m[0:1] + jnp.log(run_l[0:1])
    own_loss = jnp.sum(lt[0:1] - psc[0:1], axis=1, keepdims=True)
    metas = {}
    for k in (Y1, Y3, FRONT, BACK, SIB, FAR, Y2):
        rows = jnp.where(vis[k] > 0.5, -lt[0:1], LOWEST)
        last = lax.broadcasted_iota(I32, rows.shape, 0) == 7
        meta_out[k] = jnp.where(last, own_loss, rows)
        seen_as = SEEN_AS[k]
        cp = pltpu.make_async_remote_copy(
            src_ref=meta_out.at[k], dst_ref=meta_in.at[seen_as],
            send_sem=m_ss.at[k], recv_sem=m_rs.at[seen_as],
            device_id=where[k], device_id_type=MESH,
        )
        cp.start()
        metas[seen_as] = cp
    q_front.append(send_q(q_hbm, BACK, FRONT, hq, hq, 1))
    q_back.append(send_q(q_hbm, FRONT, BACK, hq, hq, 1))
    qa.append(send_q(q_hbm, Y1, Y3, hq, hq, 1))
    qb.append(send_q(q_hbm, Y3, Y1, 0, hq, 0))
    q_back[0].wait_recv()
    q_far = [send_q(qr.at[FRONT - 1], FAR, SIB, 0, hq, 0)]

    for k in range(8):
        @pl.loop(0, 2)
        def _(h):
            cols = pl.ds(pl.multiple_of(h * hq, hq), hq)
            factor = jnp.exp(mrow[k, 0:1, cols] - lt[0:1, cols])
            w = ebuf[k, :, cols] * factor
            if k == OWN:
                target = lax.broadcasted_iota(I32, (np_, hq), 0) == pos[0:1, cols]
                w = w - jnp.where(target, 1.0, 0.0)
            wbuf[k * np_ : (k + 1) * np_, cols] = w.astype(BF16)

    gp_ref[...] = jnp.dot(wbuf[0:np_, :], q[...], preferred_element_type=F32) * scale

    @pl.loop(0, 2)
    def _(h):
        cols = pl.ds(pl.multiple_of(h * hq, hq), hq)
        total = tn(wbuf[0:np_, cols], pall[0])
        for k in range(1, 8):
            total = total + tn(wbuf[k * np_ : (k + 1) * np_, cols], pall[k])
        gq_ref[cols, :] = total * scale

    def backward(k, first, rows):
        span = pl.ds(first, rows)
        sc = nt(pall[OWN], qr[k - 1, span, :]) * scale
        parts = []
        for b in range(blocks):
            parts.append(jnp.exp(sc[b * BLK : (b + 1) * BLK] + meta_in[k, b : b + 1, span]).astype(BF16))
        w = jnp.concatenate(parts, axis=0)
        gp_ref[...] += jnp.dot(w, qr[k - 1, span, :], preferred_element_type=F32) * scale

    loss_steps = []

    def loss_send(i, value):
        lout[i] = value
        cp = pltpu.make_async_remote_copy(
            src_ref=lout.at[i], dst_ref=lin.at[i], send_sem=l_ss.at[i], recv_sem=l_rs.at[i],
            device_id=partner[LOSS_BITS[i]], device_id_type=MESH,
        )
        cp.start()
        loss_steps.append(cp)

    def loss_next(i):
        loss_steps[i].wait_recv()
        value = lout[i] + lin[i]
        if i + 1 < len(LOSS_BITS):
            loss_send(i + 1, value)
        else:
            loss_ref[...] = value * (1.0 / (nq * n_row * n_col))

    metas[SIB].wait_recv()
    q_sib.wait_recv()
    backward(SIB, 0, hq)
    backward(SIB, hq, hq)
    metas[FRONT].wait_recv()
    backward(FRONT, 0, hq)
    metas[BACK].wait_recv()
    q_front[0].wait_recv()
    backward(BACK, 0, hq)
    metas[FAR].wait_recv()
    q_far[0].wait_recv()
    backward(FAR, 0, hq)

    qa[0].wait_recv()
    ra2 = [send_q(qr.at[Y1 - 1], Y2, Y3, i * hq // 2, hq // 2, i) for i in range(2)]
    qb[0].wait_recv()
    rb2 = [send_q(qr.at[Y3 - 1], Y2, Y1, hq + i * hq // 2, hq // 2, 2 + i) for i in range(2)]
    metas[Y1].wait_recv()
    metas[Y3].wait_recv()
    metas[Y2].wait_recv()
    spread = lax.broadcasted_iota(I32, (8, 128), 0) >= 0
    loss_at = lambda k: meta_in[k, 7:8, 0:128]
    near = loss_at(Y1) + loss_at(Y3)
    mine = meta_out[Y1, 7:8, 0:128] + loss_at(Y2)
    loss_send(0, jnp.where(spread, near + mine, 0.0))
    backward(Y1, 0, hq)
    backward(Y3, hq, hq)
    loss_next(0)
    q_back[1].wait_recv()
    q_far.append(send_q(qr.at[FRONT - 1], FAR, SIB, hq, hq, 1))
    backward(FRONT, hq, hq)
    q_front[1].wait_recv()
    backward(BACK, hq, hq)
    loss_next(1)
    q_far[1].wait_recv()
    backward(FAR, hq, hq)
    loss_next(2)
    qa[1].wait_recv()
    backward(Y1, hq, hq)
    loss_next(3)
    qb[1].wait_recv()
    backward(Y3, 0, hq)
    loss_next(4)
    for i in range(2):
        ra2[i].wait_recv()
        backward(Y2, i * hq // 2, hq // 2)
        rb2[i].wait_recv()
        backward(Y2, hq + i * hq // 2, hq // 2)

    for cp in send_p.sent + send_q.sent + list(metas.values()) + loss_steps:
        cp.wait_send()


def finish(loss, gq, gp, loss_out, gq_out, gp_out, sems):
    copies = [pltpu.make_async_copy(gq, gq_out, sems.at[0]), pltpu.make_async_copy(gp, gp_out, sems.at[1])]
    for cp in copies:
        cp.start()
    loss_out[0] = loss[0, 0]
    for cp in copies:
        cp.wait()


def local(n_row, n_col, queries, passages, positive, block_mask, roster):
    nq, width = queries.shape
    np_ = passages.shape[0]
    nb, nr = block_mask.shape[1], roster.shape[1]
    anywhere = pl.BlockSpec(memory_space=pltpu.HBM)
    inside = pl.BlockSpec(memory_space=pltpu.VMEM)
    dma = pltpu.SemaphoreType.DMA
    operands = (queries, passages, positive.reshape(1, nq), block_mask.T, roster.T)
    loss, gq, gp = pl.pallas_call(
        functools.partial(kernel, n_row, n_col),
        out_shape=(
            jax.ShapeDtypeStruct((8, 128), F32),
            jax.ShapeDtypeStruct((nq, width), F32),
            jax.ShapeDtypeStruct((np_, width), F32),
        ),
        in_specs=[anywhere] * 5,
        out_specs=(inside,) * 3,
        scratch_shapes=[
            pltpu.VMEM((nq, width), BF16),
            pltpu.VMEM((8, np_, width), BF16),
            pltpu.VMEM((7, nq, width), BF16),
            pltpu.VMEM((1, nq), I32),
            pltpu.VMEM((nb, nq), I32),
            pltpu.VMEM((nr, nq), I32),
            pltpu.VMEM((8, 8, nq), F32),
            pltpu.VMEM((8, np_, nq), F32),
            pltpu.VMEM((8 * np_, nq), BF16),
            pltpu.VMEM((8, 8, nq), F32),
            pltpu.VMEM((8, nq), F32),
            pltpu.VMEM((8, nq), F32),
            pltpu.VMEM((8, nq), F32),
            pltpu.VMEM((8, nq), F32),
            pltpu.VMEM((8, 8, nq), F32),
            pltpu.VMEM((8, 8, nq), F32),
            pltpu.VMEM((5, 8, 128), F32),
            pltpu.VMEM((5, 8, 128), F32),
            dma((5,)),
            dma((10,)),
            dma((8, 2)),
            dma((16,)),
            dma((8, 4)),
            dma((8,)),
            dma((8,)),
            dma((5,)),
            dma((5,)),
        ],
        compiler_params=pltpu.CompilerParams(
            collective_id=0, has_side_effects=True, vmem_limit_bytes=48 * 2**20
        ),
        cost_estimate=pl.CostEstimate(flops=10**10, bytes_accessed=10**7, transcendentals=4 * 10**6),
    )(*(pltpu.with_memory_space_constraint(a, pltpu.HBM) for a in operands))
    return pl.pallas_call(
        finish,
        out_shape=(
            jax.ShapeDtypeStruct((1,), F32),
            jax.ShapeDtypeStruct((nq, width), F32),
            jax.ShapeDtypeStruct((np_, width), F32),
        ),
        in_specs=[inside] * 3,
        out_specs=(pl.BlockSpec(memory_space=pltpu.SMEM), anywhere, anywhere),
        scratch_shapes=[dma((2,))],
        compiler_params=pltpu.CompilerParams(vmem_limit_bytes=4 * 2**20),
    )(loss, gq, gp)


def solution(mesh):
    whole = P(("rep", "row", "col"), None)
    return jax.shard_map(
        functools.partial(local, mesh.shape["row"], mesh.shape["col"]),
        mesh=mesh,
        in_specs=(whole, whole, P(("rep", "row", "col")), whole, whole),
        out_specs=(P("rep"), whole, whole),
        check_vma=False,
    )
```

```python
import functools

import jax
import jax.numpy as jnp
from jax import lax
from jax.experimental import pallas as pl
from jax.experimental.pallas import tpu as pltpu
from jax.sharding import PartitionSpec as P

MESH = pl.DeviceIdType.MESH
BLK = 128
LOWEST = -1e30
F32, BF16, I32 = jnp.float32, jnp.bfloat16, jnp.int32

OWN, SIB, FRONT, BACK, FAR, Y1, Y2, Y3 = range(8)
SEEN_AS = {SIB: SIB, FRONT: BACK, BACK: FRONT, FAR: FAR, Y1: Y3, Y2: Y2, Y3: Y1}


def nt(a, b):
    return lax.dot_general(a, b, (((1,), (1,)), ((), ())), preferred_element_type=F32)


def tn(a, b):
    return lax.dot_general(a, b, (((0,), (0,)), ((), ())), preferred_element_type=F32)


def kernel(
    n_row, n_col, n_z,
    q_hbm, p_hbm, pos_hbm, bm_hbm, ro_hbm,
    loss_ref, gq_ref, gp_ref,
    q, pall, qr, pos, bm, ro, vis, ebuf, wbuf, mrow, run_m, run_l, lt, psc, meta_out, meta_in, zin, xin,
    loc_s, p_ss, p_rs, q_ss, q_rs, m_ss, m_rs, z_ss, z_rs, x_ss, x_rs, y_in, z_in,
):
    nq, width = q.shape
    np_ = pall.shape[1]
    blocks = np_ // BLK
    scale = width ** (-0.5)
    hq, hp = nq // 2, np_ // 2
    r, c = lax.axis_index("row"), lax.axis_index("col")
    odd = lax.rem(r, 2)
    s = 1 - 2 * odd

    def at_row(o):
        return {"row": lax.rem(r + o + n_row, n_row), "col": c}

    def at_col(o):
        return {"row": r, "col": lax.rem(c + o + n_col, n_col)}

    where = {
        SIB: at_row(s), FRONT: at_row(2 * s), BACK: at_row(-2 * s), FAR: at_row(-s),
        Y1: at_col(-1), Y2: at_col(-2), Y3: at_col(1),
    }
    z = lax.rem(lax.div(r, 2), n_z)
    side = lax.div(r, 2 * n_z)
    along_z = {i: {"row": side * 2 * n_z + 2 * lax.rem(z + i, n_z) + odd, "col": c} for i in range(1, n_z)}
    over_x = (1 - side) * 2 * n_z + 2 * z
    same_z = {1: where[SIB], 2: {"row": over_x + odd, "col": c}, 3: {"row": over_x + 1 - odd, "col": c}}

    barrier = pltpu.get_barrier_semaphore()
    chip = r - odd
    even_core, odd_core = {"row": chip, "col": c}, {"row": chip + 1, "col": c}
    for o in range(1, n_col):
        pl.semaphore_signal(
            barrier, inc=1, device_id={"row": chip, "col": lax.rem(c + o, n_col)}, device_id_type=MESH
        )

    @pl.when(odd == 1)
    def _():
        pl.semaphore_signal(barrier, inc=1, device_id=even_core, device_id_type=MESH)

    chips = [lax.rem(chip + 2, n_row), lax.rem(chip + n_row - 2, n_row), over_x]
    chips += [to["row"] - odd for to in along_z.values()]
    for there in chips:
        pl.semaphore_signal(barrier, inc=1, device_id={"row": there + 1, "col": c}, device_id_type=MESH)

    loads = [
        pltpu.make_async_copy(src, dst, loc_s.at[i])
        for i, (src, dst) in enumerate(
            ((q_hbm, q), (p_hbm, pall.at[OWN]), (bm_hbm, bm), (ro_hbm, ro), (pos_hbm, pos))
        )
    ]
    for cp in loads:
        cp.start()

    @pl.when(odd == 0)
    def _():
        pl.semaphore_wait(barrier, 2 * (n_col - 1) + 1)
        pl.semaphore_signal(y_in, inc=1, device_id=odd_core, device_id_type=MESH)

    @pl.when(odd == 1)
    def _():
        pl.semaphore_wait(y_in, 1)

    class Sender:
        def __init__(self, ss, rs, land):
            self.ss, self.rs, self.land, self.n, self.sent = ss, rs, land, 0, []

        def __call__(self, src, slot, to, first, rows, mark):
            cp = pltpu.make_async_remote_copy(
                src_ref=src.at[pl.ds(first, rows)],
                dst_ref=self.land(slot).at[pl.ds(first, rows)],
                send_sem=self.ss.at[self.n],
                recv_sem=self.rs.at[slot, mark],
                device_id=where[to],
                device_id_type=MESH,
            )
            self.n += 1
            self.sent.append(cp)
            cp.start()
            return cp

    send_p = Sender(p_ss, p_rs, lambda k: pall.at[k])
    send_q = Sender(q_ss, q_rs, lambda k: qr.at[k - 1])

    pa0 = send_p(p_hbm, Y1, Y3, 0, hp, 0)
    pb1 = send_p(p_hbm, Y3, Y1, hp, hp, 1)
    pa1 = send_p(p_hbm, Y1, Y3, hp, hp, 1)
    pb0 = send_p(p_hbm, Y3, Y1, 0, hp, 0)
    p_sib = send_p(p_hbm, SIB, SIB, 0, np_, 0)
    q_sib = send_q(q_hbm, SIB, SIB, 0, nq, 0)

    @pl.when(odd == 1)
    def _():
        pl.semaphore_wait(barrier, 2 * len(chips))
        pl.semaphore_signal(z_in, inc=1, device_id=even_core, device_id_type=MESH)

    @pl.when(odd == 0)
    def _():
        pl.semaphore_wait(z_in, 1)

    p_front = send_p(p_hbm, BACK, FRONT, 0, np_, 0)
    p_back = send_p(p_hbm, FRONT, BACK, 0, np_, 0)
    qz = nq * 5 // 8
    q_front = [send_q(q_hbm, BACK, FRONT, 0, qz, 0)]
    q_back = [send_q(q_hbm, FRONT, BACK, 0, qz, 0)]

    for cp in loads:
        cp.wait()
    row_i = lax.broadcasted_iota(I32, (64, 1), 0)
    slot_i, block_i = lax.shift_right_logical(row_i, 3), lax.bitwise_and(row_i, 7)
    up = jnp.where(odd == 0, jnp.int32(1), jnp.int32(0))
    group = jnp.where(
        slot_i == SIB, 2 + up,
        jnp.where(slot_i == FRONT, 1 + 3 * up, jnp.where(slot_i == BACK, 4 - 3 * up, jnp.where(slot_i == FAR, 3 - up, 0))),
    )
    nb = bm.shape[0]
    wanted = jnp.where((slot_i <= FAR) & (block_i < blocks), group * blocks + block_i, -1)
    pick = jnp.where(lax.broadcasted_iota(I32, (64, nb), 1) == wanted, 1.0, 0.0).astype(BF16)
    seen = jnp.dot(pick, bm[...].astype(F32).astype(BF16), preferred_element_type=F32)
    nr = ro.shape[0]
    pick_r = jnp.where(lax.broadcasted_iota(I32, (64, nr), 1) == slot_i - Y1, 1.0, 0.0).astype(BF16)
    listed = jnp.dot(pick_r, ro[...].astype(F32).astype(BF16), preferred_element_type=F32)
    in_roster = jnp.where(jnp.abs(listed - block_i.astype(F32)) < 0.5, 1.0, 0.0)
    seen = jnp.where(slot_i >= Y1, in_roster, seen)
    pos_row = pos[...]
    own_block = jnp.where((slot_i == OWN) & (lax.shift_right_logical(pos_row, 7) == block_i), 1.0, 0.0)
    seen = jnp.maximum(seen, own_block)
    for k in range(8):
        vis[k] = seen[8 * k : 8 * k + 8]

    run_m[...] = jnp.full(run_m.shape, LOWEST, F32)
    run_l[...] = jnp.zeros(run_l.shape, F32)

    def forward(k):
        @pl.loop(0, 2)
        def _(h):
            cols = pl.ds(pl.multiple_of(h * hq, hq), hq)
            sc = nt(pall[k], q[cols, :]) * scale
            v = vis[k, :, cols]
            m_old = run_m[0:1, cols]
            m_new = m_old
            for b in range(blocks):
                top = jnp.max(sc[b * BLK : (b + 1) * BLK], axis=0, keepdims=True)
                m_new = jnp.maximum(m_new, jnp.where(v[b : b + 1] > 0.5, top, LOWEST))
            total = run_l[0:1, cols] * jnp.exp(m_old - m_new)
            for b in range(blocks):
                bias = jnp.where(v[b : b + 1] > 0.5, -m_new, LOWEST)
                e = jnp.exp(sc[b * BLK : (b + 1) * BLK] + bias)
                total = total + jnp.sum(e, axis=0, keepdims=True)
                ebuf[k, b * BLK : (b + 1) * BLK, cols] = e
            if k == OWN:
                target = lax.broadcasted_iota(I32, (np_, hq), 0) == pos[0:1, cols]
                psc[0:1, cols] = jnp.sum(jnp.where(target, sc, 0.0), axis=0, keepdims=True)
            run_m[0:1, cols] = m_new
            run_l[0:1, cols] = total
            mrow[k, 0:1, cols] = m_new

    forward(OWN)
    p_sib.wait_recv()
    forward(SIB)
    pa0.wait_recv()
    ra = send_p(pall.at[Y1], Y2, Y3, 0, hp, 0)
    pb1.wait_recv()
    rb = send_p(pall.at[Y3], Y2, Y1, hp, hp, 1)
    pa1.wait_recv()
    pb0.wait_recv()
    qe, qs = nq // 4, nq // 8
    qa = [send_q(q_hbm, Y1, Y3, 0, qe, 0)]
    qb = [send_q(q_hbm, Y3, Y1, nq - qe, qe, 0)]
    forward(Y1)
    forward(Y3)
    p_back.wait_recv()
    p_far = send_p(pall.at[FRONT], FAR, SIB, 0, np_, 0)
    p_front.wait_recv()
    forward(FRONT)
    forward(BACK)
    ra.wait_recv()
    rb.wait_recv()
    forward(Y2)
    p_far.wait_recv()
    forward(FAR)

    lt[0:1] = run_m[0:1] + jnp.log(run_l[0:1])
    own_loss = jnp.sum(lt[0:1] - psc[0:1], axis=1, keepdims=True)
    metas = {}
    for k in (Y1, Y3, FRONT, BACK, SIB, FAR, Y2):
        rows = jnp.where(vis[k] > 0.5, -lt[0:1], LOWEST)
        last = lax.broadcasted_iota(I32, rows.shape, 0) == 7
        meta_out[k] = jnp.where(last, own_loss, rows)
        seen_as = SEEN_AS[k]
        cp = pltpu.make_async_remote_copy(
            src_ref=meta_out.at[k], dst_ref=meta_in.at[seen_as],
            send_sem=m_ss.at[k], recv_sem=m_rs.at[seen_as],
            device_id=where[k], device_id_type=MESH,
        )
        cp.start()
        metas[seen_as] = cp
    qa += [send_q(q_hbm, Y1, Y3, qe, qe, 1), send_q(q_hbm, Y1, Y3, hq, hq, 2)]
    qb += [send_q(q_hbm, Y3, Y1, hq, qe, 1), send_q(q_hbm, Y3, Y1, 0, hq, 2)]
    q_back[0].wait_recv()
    q_far = [send_q(qr.at[FRONT - 1], FAR, SIB, 0, qz, 0)]

    for k in range(8):
        @pl.loop(0, 2)
        def _(h):
            cols = pl.ds(pl.multiple_of(h * hq, hq), hq)
            factor = jnp.exp(mrow[k, 0:1, cols] - lt[0:1, cols])
            w = ebuf[k, :, cols] * factor
            if k == OWN:
                target = lax.broadcasted_iota(I32, (np_, hq), 0) == pos[0:1, cols]
                w = w - jnp.where(target, 1.0, 0.0)
            wbuf[k * np_ : (k + 1) * np_, cols] = w.astype(BF16)

    gp_ref[...] = jnp.dot(wbuf[0:np_, :], q[...], preferred_element_type=F32) * scale

    @pl.loop(0, 2)
    def _(h):
        cols = pl.ds(pl.multiple_of(h * hq, hq), hq)
        total = tn(wbuf[0:np_, cols], pall[0])
        for k in range(1, 8):
            total = total + tn(wbuf[k * np_ : (k + 1) * np_, cols], pall[k])
        gq_ref[cols, :] = total * scale

    def backward(k, first, rows):
        span = pl.ds(first, rows)
        sc = nt(pall[OWN], qr[k - 1, span, :]) * scale
        parts = []
        for b in range(blocks):
            parts.append(jnp.exp(sc[b * BLK : (b + 1) * BLK] + meta_in[k, b : b + 1, span]).astype(BF16))
        w = jnp.concatenate(parts, axis=0)
        gp_ref[...] += jnp.dot(w, qr[k - 1, span, :], preferred_element_type=F32) * scale

    loss_at = lambda k: meta_in[k, 7:8, 0:128]
    for k in (Y1, Y3, Y2):
        metas[k].wait_recv()
    near = loss_at(Y1) + loss_at(Y3)
    mine = meta_out[Y1, 7:8, 0:128] + loss_at(Y2)
    zin[0] = jnp.broadcast_to(near + mine, (8, 128))

    def spread(buf, ss, rs, partners):
        copies = []
        for i, to in partners.items():
            cp = pltpu.make_async_remote_copy(
                src_ref=buf.at[0], dst_ref=buf.at[i], send_sem=ss.at[i], recv_sem=rs.at[i],
                device_id=to, device_id_type=MESH,
            )
            cp.start()
            copies.append(cp)
        return copies

    loss_z = spread(zin, z_ss, z_rs, along_z)
    q_front.append(send_q(q_hbm, BACK, FRONT, qz, nq - qz, 1))
    q_back.append(send_q(q_hbm, FRONT, BACK, qz, nq - qz, 1))

    qa[0].wait_recv()
    ra2 = [send_q(qr.at[Y1 - 1], Y2, Y3, 0, qe, 0)]
    qb[0].wait_recv()
    rb2 = [send_q(qr.at[Y3 - 1], Y2, Y1, nq - qe, qe, 3)]
    metas[SIB].wait_recv()
    q_sib.wait_recv()
    backward(SIB, 0, hq)
    backward(SIB, hq, hq)
    qa[1].wait_recv()
    ra2 += [send_q(qr.at[Y1 - 1], Y2, Y3, qe + i * qs, qs, 1 + i) for i in range(2)]
    qb[1].wait_recv()
    rb2 += [send_q(qr.at[Y3 - 1], Y2, Y1, nq - qe - (i + 1) * qs, qs, 4 + i) for i in range(2)]
    backward(Y1, 0, hq)
    backward(Y3, hq, hq)
    metas[FRONT].wait_recv()
    backward(FRONT, 0, hq)
    metas[BACK].wait_recv()
    q_front[0].wait_recv()
    backward(BACK, 0, hq)
    metas[FAR].wait_recv()
    q_far[0].wait_recv()
    backward(FAR, 0, hq)
    for cp in loss_z:
        cp.wait_recv()
    total = zin[z]
    for i in range(1, n_z):
        total = total + zin[lax.rem(z + n_z - i, n_z)]
    xin[0] = total
    loss_x = spread(xin, x_ss, x_rs, same_z)
    q_back[1].wait_recv()
    q_far.append(send_q(qr.at[FRONT - 1], FAR, SIB, qz, nq - qz, 1))
    backward(FRONT, hq, hq)
    q_front[1].wait_recv()
    backward(BACK, hq, hq)
    qa[2].wait_recv()
    backward(Y1, hq, hq)
    qb[2].wait_recv()
    backward(Y3, 0, hq)
    q_far[1].wait_recv()
    backward(FAR, hq, hq)
    ra2[0].wait_recv()
    backward(Y2, 0, qe)
    rb2[0].wait_recv()
    backward(Y2, nq - qe, qe)
    for cp in loss_x:
        cp.wait_recv()
    loss_ref[...] = ((xin[0] + xin[1]) + (xin[2] + xin[3])) * (1.0 / (nq * n_row * n_col))
    ra2[1].wait_recv()
    rb2[1].wait_recv()
    backward(Y2, qe, qs)
    backward(Y2, nq - qe - qs, qs)
    ra2[2].wait_recv()
    rb2[2].wait_recv()
    backward(Y2, hq - qs, 2 * qs)

    for cp in send_p.sent + send_q.sent + list(metas.values()) + loss_z + loss_x:
        cp.wait_send()


def finish(loss, gq, gp, loss_out, gq_out, gp_out, sems):
    copies = [pltpu.make_async_copy(gq, gq_out, sems.at[0]), pltpu.make_async_copy(gp, gp_out, sems.at[1])]
    for cp in copies:
        cp.start()
    loss_out[0] = loss[0, 0]
    for cp in copies:
        cp.wait()


def local(n_row, n_col, queries, passages, positive, block_mask, roster):
    nq, width = queries.shape
    np_ = passages.shape[0]
    n_z = n_row // 4
    nb, nr = block_mask.shape[1], roster.shape[1]
    anywhere = pl.BlockSpec(memory_space=pltpu.HBM)
    inside = pl.BlockSpec(memory_space=pltpu.VMEM)
    dma = pltpu.SemaphoreType.DMA
    operands = (queries, passages, positive.reshape(1, nq), block_mask.T, roster.T)
    loss, gq, gp = pl.pallas_call(
        functools.partial(kernel, n_row, n_col, n_z),
        out_shape=(
            jax.ShapeDtypeStruct((8, 128), F32),
            jax.ShapeDtypeStruct((nq, width), F32),
            jax.ShapeDtypeStruct((np_, width), F32),
        ),
        in_specs=[anywhere] * 5,
        out_specs=(inside,) * 3,
        scratch_shapes=[
            pltpu.VMEM((nq, width), BF16),
            pltpu.VMEM((8, np_, width), BF16),
            pltpu.VMEM((7, nq, width), BF16),
            pltpu.VMEM((1, nq), I32),
            pltpu.VMEM((nb, nq), I32),
            pltpu.VMEM((nr, nq), I32),
            pltpu.VMEM((8, 8, nq), F32),
            pltpu.VMEM((8, np_, nq), F32),
            pltpu.VMEM((8 * np_, nq), BF16),
            pltpu.VMEM((8, 8, nq), F32),
            pltpu.VMEM((8, nq), F32),
            pltpu.VMEM((8, nq), F32),
            pltpu.VMEM((8, nq), F32),
            pltpu.VMEM((8, nq), F32),
            pltpu.VMEM((8, 8, nq), F32),
            pltpu.VMEM((8, 8, nq), F32),
            pltpu.VMEM((n_z, 8, 128), F32),
            pltpu.VMEM((4, 8, 128), F32),
            dma((5,)),
            dma((10,)),
            dma((8, 2)),
            dma((19,)),
            dma((8, 6)),
            dma((8,)),
            dma((8,)),
            dma((n_z,)),
            dma((n_z,)),
            dma((4,)),
            dma((4,)),
            pltpu.SemaphoreType.REGULAR,
            pltpu.SemaphoreType.REGULAR,
        ],
        compiler_params=pltpu.CompilerParams(
            collective_id=0, has_side_effects=True, vmem_limit_bytes=48 * 2**20
        ),
        cost_estimate=pl.CostEstimate(flops=10**10, bytes_accessed=10**7, transcendentals=4 * 10**6),
    )(*(pltpu.with_memory_space_constraint(a, pltpu.HBM) for a in operands))
    return pl.pallas_call(
        finish,
        out_shape=(
            jax.ShapeDtypeStruct((1,), F32),
            jax.ShapeDtypeStruct((nq, width), F32),
            jax.ShapeDtypeStruct((np_, width), F32),
        ),
        in_specs=[inside] * 3,
        out_specs=(pl.BlockSpec(memory_space=pltpu.SMEM), anywhere, anywhere),
        scratch_shapes=[dma((2,))],
        compiler_params=pltpu.CompilerParams(vmem_limit_bytes=4 * 2**20),
    )(loss, gq, gp)


def solution(mesh):
    whole = P(("rep", "row", "col"), None)
    return jax.shard_map(
        functools.partial(local, mesh.shape["row"], mesh.shape["col"]),
        mesh=mesh,
        in_specs=(whole, whole, P(("rep", "row", "col")), whole, whole),
        out_specs=(P("rep"), whole, whole),
        check_vma=False,
    )
```

```python
import functools

import jax
import jax.numpy as jnp
from jax import lax
from jax.experimental import pallas as pl
from jax.experimental.pallas import tpu as pltpu
from jax.sharding import PartitionSpec as P

MESH = pl.DeviceIdType.MESH
BLK = 128
LOWEST = -1e30
F32, BF16, I32 = jnp.float32, jnp.bfloat16, jnp.int32

OWN, SIB, FRONT, BACK, FAR, Y1, Y2, Y3 = range(8)
SEEN_AS = {SIB: SIB, FRONT: BACK, BACK: FRONT, FAR: FAR, Y1: Y3, Y2: Y2, Y3: Y1}


def nt(a, b):
    return lax.dot_general(a, b, (((1,), (1,)), ((), ())), preferred_element_type=F32)


def tn(a, b):
    return lax.dot_general(a, b, (((0,), (0,)), ((), ())), preferred_element_type=F32)


def kernel(
    n_row, n_col, n_z,
    q_hbm, p_hbm, pos_hbm, bm_hbm, ro_hbm,
    loss_ref, gq_ref, gp_ref,
    q, pall, qr, pos, bm, ro, vis, ebuf, wbuf, mrow, run_m, run_l, lt, psc, meta_out, meta_in, zin, xin,
    loc_s, p_ss, p_rs, q_ss, q_rs, m_ss, m_rs, z_ss, z_rs, x_ss, x_rs, y_in, z_in,
):
    nq, width = q.shape
    np_ = pall.shape[1]
    blocks = np_ // BLK
    scale = width ** (-0.5)
    hq, hp = nq // 2, np_ // 2
    r, c = lax.axis_index("row"), lax.axis_index("col")
    odd = lax.rem(r, 2)
    s = 1 - 2 * odd

    def at_row(o):
        return {"row": lax.rem(r + o + n_row, n_row), "col": c}

    def at_col(o):
        return {"row": r, "col": lax.rem(c + o + n_col, n_col)}

    where = {
        SIB: at_row(s), FRONT: at_row(2 * s), BACK: at_row(-2 * s), FAR: at_row(-s),
        Y1: at_col(-1), Y2: at_col(-2), Y3: at_col(1),
    }
    z = lax.rem(lax.div(r, 2), n_z)
    side = lax.div(r, 2 * n_z)
    along_z = {i: {"row": side * 2 * n_z + 2 * lax.rem(z + i, n_z) + odd, "col": c} for i in range(1, n_z)}
    over_x = (1 - side) * 2 * n_z + 2 * z
    same_z = {1: where[SIB], 2: {"row": over_x + odd, "col": c}, 3: {"row": over_x + 1 - odd, "col": c}}

    barrier = pltpu.get_barrier_semaphore()
    chip = r - odd
    even_core, odd_core = {"row": chip, "col": c}, {"row": chip + 1, "col": c}
    for o in range(1, n_col):
        pl.semaphore_signal(
            barrier, inc=1, device_id={"row": chip, "col": lax.rem(c + o, n_col)}, device_id_type=MESH
        )

    @pl.when(odd == 1)
    def _():
        pl.semaphore_signal(barrier, inc=1, device_id=even_core, device_id_type=MESH)

    chips = [lax.rem(chip + 2, n_row), lax.rem(chip + n_row - 2, n_row), over_x]
    chips += [to["row"] - odd for to in along_z.values()]
    for there in chips:
        pl.semaphore_signal(barrier, inc=1, device_id={"row": there + 1, "col": c}, device_id_type=MESH)

    loads = [
        pltpu.make_async_copy(src, dst, loc_s.at[i])
        for i, (src, dst) in enumerate(
            ((q_hbm, q), (p_hbm, pall.at[OWN]), (bm_hbm, bm), (ro_hbm, ro), (pos_hbm, pos))
        )
    ]
    for cp in loads:
        cp.start()

    @pl.when(odd == 0)
    def _():
        pl.semaphore_wait(barrier, 2 * (n_col - 1) + 1)
        pl.semaphore_signal(y_in, inc=1, device_id=odd_core, device_id_type=MESH)

    @pl.when(odd == 1)
    def _():
        pl.semaphore_wait(y_in, 1)

    class Sender:
        def __init__(self, ss, rs, land):
            self.ss, self.rs, self.land, self.n, self.sent = ss, rs, land, 0, []

        def __call__(self, src, slot, to, first, rows, mark):
            cp = pltpu.make_async_remote_copy(
                src_ref=src.at[pl.ds(first, rows)],
                dst_ref=self.land(slot).at[pl.ds(first, rows)],
                send_sem=self.ss.at[self.n],
                recv_sem=self.rs.at[slot, mark],
                device_id=where[to],
                device_id_type=MESH,
            )
            self.n += 1
            self.sent.append(cp)
            cp.start()
            return cp

    send_p = Sender(p_ss, p_rs, lambda k: pall.at[k])
    send_q = Sender(q_ss, q_rs, lambda k: qr.at[k - 1])

    pa0 = send_p(p_hbm, Y1, Y3, 0, hp, 0)
    pb1 = send_p(p_hbm, Y3, Y1, hp, hp, 1)
    pa1 = send_p(p_hbm, Y1, Y3, hp, hp, 1)
    pb0 = send_p(p_hbm, Y3, Y1, 0, hp, 0)
    p_sib = send_p(p_hbm, SIB, SIB, 0, np_, 0)
    q_sib = send_q(q_hbm, SIB, SIB, 0, nq, 0)

    @pl.when(odd == 1)
    def _():
        pl.semaphore_wait(barrier, 2 * len(chips))
        pl.semaphore_signal(z_in, inc=1, device_id=even_core, device_id_type=MESH)

    @pl.when(odd == 0)
    def _():
        pl.semaphore_wait(z_in, 1)

    p_front = send_p(p_hbm, BACK, FRONT, 0, np_, 0)
    p_back = send_p(p_hbm, FRONT, BACK, 0, np_, 0)
    qz = nq * 5 // 8
    q_front = [send_q(q_hbm, BACK, FRONT, 0, qz, 0)]
    q_back = [send_q(q_hbm, FRONT, BACK, 0, qz, 0)]

    for cp in loads:
        cp.wait()
    row_i = lax.broadcasted_iota(I32, (64, 1), 0)
    slot_i, block_i = lax.shift_right_logical(row_i, 3), lax.bitwise_and(row_i, 7)
    up = jnp.where(odd == 0, jnp.int32(1), jnp.int32(0))
    group = jnp.where(
        slot_i == SIB, 2 + up,
        jnp.where(slot_i == FRONT, 1 + 3 * up, jnp.where(slot_i == BACK, 4 - 3 * up, jnp.where(slot_i == FAR, 3 - up, 0))),
    )
    nb = bm.shape[0]
    wanted = jnp.where((slot_i <= FAR) & (block_i < blocks), group * blocks + block_i, -1)
    pick = jnp.where(lax.broadcasted_iota(I32, (64, nb), 1) == wanted, 1.0, 0.0).astype(BF16)
    seen = jnp.dot(pick, bm[...].astype(F32).astype(BF16), preferred_element_type=F32)
    nr = ro.shape[0]
    pick_r = jnp.where(lax.broadcasted_iota(I32, (64, nr), 1) == slot_i - Y1, 1.0, 0.0).astype(BF16)
    listed = jnp.dot(pick_r, ro[...].astype(F32).astype(BF16), preferred_element_type=F32)
    in_roster = jnp.where(jnp.abs(listed - block_i.astype(F32)) < 0.5, 1.0, 0.0)
    seen = jnp.where(slot_i >= Y1, in_roster, seen)
    pos_row = pos[...]
    own_block = jnp.where((slot_i == OWN) & (lax.shift_right_logical(pos_row, 7) == block_i), 1.0, 0.0)
    seen = jnp.maximum(seen, own_block)
    for k in range(8):
        vis[k] = seen[8 * k : 8 * k + 8]

    run_m[...] = jnp.full(run_m.shape, LOWEST, F32)
    run_l[...] = jnp.zeros(run_l.shape, F32)

    def forward(k):
        @pl.loop(0, 2)
        def _(h):
            cols = pl.ds(pl.multiple_of(h * hq, hq), hq)
            sc = nt(pall[k], q[cols, :]) * scale
            v = vis[k, :, cols]
            m_old = run_m[0:1, cols]
            m_new = m_old
            for b in range(blocks):
                top = jnp.max(sc[b * BLK : (b + 1) * BLK], axis=0, keepdims=True)
                m_new = jnp.maximum(m_new, jnp.where(v[b : b + 1] > 0.5, top, LOWEST))
            total = run_l[0:1, cols] * jnp.exp(m_old - m_new)
            for b in range(blocks):
                bias = jnp.where(v[b : b + 1] > 0.5, -m_new, LOWEST)
                e = jnp.exp(sc[b * BLK : (b + 1) * BLK] + bias)
                total = total + jnp.sum(e, axis=0, keepdims=True)
                ebuf[k, b * BLK : (b + 1) * BLK, cols] = e
            if k == OWN:
                target = lax.broadcasted_iota(I32, (np_, hq), 0) == pos[0:1, cols]
                psc[0:1, cols] = jnp.sum(jnp.where(target, sc, 0.0), axis=0, keepdims=True)
            run_m[0:1, cols] = m_new
            run_l[0:1, cols] = total
            mrow[k, 0:1, cols] = m_new

    forward(OWN)
    p_sib.wait_recv()
    forward(SIB)
    pa0.wait_recv()
    ra = send_p(pall.at[Y1], Y2, Y3, 0, hp, 0)
    pb1.wait_recv()
    rb = send_p(pall.at[Y3], Y2, Y1, hp, hp, 1)
    pa1.wait_recv()
    pb0.wait_recv()
    qe, qs, q0 = nq // 4, nq // 8, nq * 3 // 8
    qa = [send_q(q_hbm, Y1, Y3, 0, q0, 0), send_q(q_hbm, Y1, Y3, q0, hq - q0, 1)]
    qb = [send_q(q_hbm, Y3, Y1, nq - q0, q0, 0), send_q(q_hbm, Y3, Y1, hq, hq - q0, 1)]
    forward(Y1)
    forward(Y3)
    p_back.wait_recv()
    p_far = send_p(pall.at[FRONT], FAR, SIB, 0, np_, 0)
    p_front.wait_recv()
    forward(FRONT)
    forward(BACK)
    p_far.wait_recv()
    forward(FAR)
    ra.wait_recv()
    rb.wait_recv()
    forward(Y2)

    lt[0:1] = run_m[0:1] + jnp.log(run_l[0:1])
    own_loss = jnp.sum(lt[0:1] - psc[0:1], axis=1, keepdims=True)
    metas = {}
    for k in (Y1, Y3, Y2, FRONT, BACK, FAR, SIB):
        rows = jnp.where(vis[k] > 0.5, -lt[0:1], LOWEST)
        last = lax.broadcasted_iota(I32, rows.shape, 0) == 7
        meta_out[k] = jnp.where(last, own_loss, rows)
        seen_as = SEEN_AS[k]
        cp = pltpu.make_async_remote_copy(
            src_ref=meta_out.at[k], dst_ref=meta_in.at[seen_as],
            send_sem=m_ss.at[k], recv_sem=m_rs.at[seen_as],
            device_id=where[k], device_id_type=MESH,
        )
        cp.start()
        metas[seen_as] = cp
    q_front.append(send_q(q_hbm, BACK, FRONT, qz, nq - qz, 1))
    q_back.append(send_q(q_hbm, FRONT, BACK, qz, nq - qz, 1))
    qa.append(send_q(q_hbm, Y1, Y3, hq, hq, 2))
    qb.append(send_q(q_hbm, Y3, Y1, 0, hq, 2))

    for k in range(8):
        @pl.loop(0, 2)
        def _(h):
            cols = pl.ds(pl.multiple_of(h * hq, hq), hq)
            factor = jnp.exp(mrow[k, 0:1, cols] - lt[0:1, cols])
            w = ebuf[k, :, cols] * factor
            if k == OWN:
                target = lax.broadcasted_iota(I32, (np_, hq), 0) == pos[0:1, cols]
                w = w - jnp.where(target, 1.0, 0.0)
            wbuf[k * np_ : (k + 1) * np_, cols] = w.astype(BF16)

    gp_ref[...] = jnp.dot(wbuf[0:np_, :], q[...], preferred_element_type=F32) * scale

    def own_gradient(first):
        cols = pl.ds(first, hq)
        total = tn(wbuf[0:np_, cols], pall[0])
        for k in range(1, 8):
            total = total + tn(wbuf[k * np_ : (k + 1) * np_, cols], pall[k])
        gq_ref[cols, :] = total * scale

    own_gradient(0)

    def backward(k, first, rows):
        span = pl.ds(first, rows)
        sc = nt(pall[OWN], qr[k - 1, span, :]) * scale
        parts = []
        for b in range(blocks):
            parts.append(jnp.exp(sc[b * BLK : (b + 1) * BLK] + meta_in[k, b : b + 1, span]).astype(BF16))
        w = jnp.concatenate(parts, axis=0)
        gp_ref[...] += jnp.dot(w, qr[k - 1, span, :], preferred_element_type=F32) * scale

    loss_at = lambda k: meta_in[k, 7:8, 0:128]
    for k in (Y1, Y3, Y2):
        metas[k].wait_recv()
    near = loss_at(Y1) + loss_at(Y3)
    mine = meta_out[Y1, 7:8, 0:128] + loss_at(Y2)
    zin[0] = jnp.broadcast_to(near + mine, (8, 128))

    def spread(buf, ss, rs, partners):
        copies = []
        for i, to in partners.items():
            cp = pltpu.make_async_remote_copy(
                src_ref=buf.at[0], dst_ref=buf.at[i], send_sem=ss.at[i], recv_sem=rs.at[i],
                device_id=to, device_id_type=MESH,
            )
            cp.start()
            copies.append(cp)
        return copies

    loss_z = spread(zin, z_ss, z_rs, along_z)

    qa[0].wait_recv()
    ra2 = [send_q(qr.at[Y1 - 1], Y2, Y3, 0, qe, 0)]
    qb[0].wait_recv()
    rb2 = [send_q(qr.at[Y3 - 1], Y2, Y1, nq - qe, qe, 3)]
    own_gradient(hq)
    qa[1].wait_recv()
    ra2 += [send_q(qr.at[Y1 - 1], Y2, Y3, qe + i * qs, qs, 1 + i) for i in range(2)]
    qb[1].wait_recv()
    rb2 += [send_q(qr.at[Y3 - 1], Y2, Y1, nq - qe - (i + 1) * qs, qs, 4 + i) for i in range(2)]
    metas[SIB].wait_recv()
    q_sib.wait_recv()
    backward(SIB, 0, hq)
    backward(SIB, hq, hq)
    backward(Y1, 0, hq)
    backward(Y3, hq, hq)
    q_back[0].wait_recv()
    q_far = [send_q(qr.at[FRONT - 1], FAR, SIB, 0, qz, 0)]
    metas[FRONT].wait_recv()
    backward(FRONT, 0, hq)
    metas[BACK].wait_recv()
    q_front[0].wait_recv()
    backward(BACK, 0, hq)
    metas[FAR].wait_recv()
    q_far[0].wait_recv()
    backward(FAR, 0, hq)
    for cp in loss_z:
        cp.wait_recv()
    total = zin[z]
    for i in range(1, n_z):
        total = total + zin[lax.rem(z + n_z - i, n_z)]
    xin[0] = total
    loss_x = spread(xin, x_ss, x_rs, same_z)
    q_back[1].wait_recv()
    q_far.append(send_q(qr.at[FRONT - 1], FAR, SIB, qz, nq - qz, 1))
    backward(FRONT, hq, hq)
    q_front[1].wait_recv()
    backward(BACK, hq, hq)
    qa[2].wait_recv()
    backward(Y1, hq, hq)
    qb[2].wait_recv()
    backward(Y3, 0, hq)
    q_far[1].wait_recv()
    backward(FAR, hq, hq)
    ra2[0].wait_recv()
    backward(Y2, 0, qe)
    rb2[0].wait_recv()
    backward(Y2, nq - qe, qe)
    for cp in loss_x:
        cp.wait_recv()
    loss_ref[...] = ((xin[0] + xin[1]) + (xin[2] + xin[3])) * (1.0 / (nq * n_row * n_col))
    ra2[1].wait_recv()
    rb2[1].wait_recv()
    backward(Y2, qe, qs)
    backward(Y2, nq - qe - qs, qs)
    ra2[2].wait_recv()
    rb2[2].wait_recv()
    backward(Y2, hq - qs, 2 * qs)

    for cp in send_p.sent + send_q.sent + list(metas.values()) + loss_z + loss_x:
        cp.wait_send()


def finish(loss, gq, gp, loss_out, gq_out, gp_out, sems):
    copies = [pltpu.make_async_copy(gq, gq_out, sems.at[0]), pltpu.make_async_copy(gp, gp_out, sems.at[1])]
    for cp in copies:
        cp.start()
    loss_out[...] = loss[0, 0:1]
    for cp in copies:
        cp.wait()


def local(n_row, n_col, queries, passages, positive, block_mask, roster):
    nq, width = queries.shape
    np_ = passages.shape[0]
    n_z = n_row // 4
    nb, nr = block_mask.shape[1], roster.shape[1]
    anywhere = pl.BlockSpec(memory_space=pltpu.HBM)
    inside = pl.BlockSpec(memory_space=pltpu.VMEM)
    dma = pltpu.SemaphoreType.DMA
    operands = (queries, passages, positive.reshape(1, nq), block_mask.T, roster.T)
    loss, gq, gp = pl.pallas_call(
        functools.partial(kernel, n_row, n_col, n_z),
        out_shape=(
            jax.ShapeDtypeStruct((8, 128), F32),
            jax.ShapeDtypeStruct((nq, width), F32),
            jax.ShapeDtypeStruct((np_, width), F32),
        ),
        in_specs=[anywhere] * 5,
        out_specs=(inside,) * 3,
        scratch_shapes=[
            pltpu.VMEM((nq, width), BF16),
            pltpu.VMEM((8, np_, width), BF16),
            pltpu.VMEM((7, nq, width), BF16),
            pltpu.VMEM((1, nq), I32),
            pltpu.VMEM((nb, nq), I32),
            pltpu.VMEM((nr, nq), I32),
            pltpu.VMEM((8, 8, nq), F32),
            pltpu.VMEM((8, np_, nq), F32),
            pltpu.VMEM((8 * np_, nq), BF16),
            pltpu.VMEM((8, 8, nq), F32),
            pltpu.VMEM((8, nq), F32),
            pltpu.VMEM((8, nq), F32),
            pltpu.VMEM((8, nq), F32),
            pltpu.VMEM((8, nq), F32),
            pltpu.VMEM((8, 8, nq), F32),
            pltpu.VMEM((8, 8, nq), F32),
            pltpu.VMEM((n_z, 8, 128), F32),
            pltpu.VMEM((4, 8, 128), F32),
            dma((5,)),
            dma((10,)),
            dma((8, 2)),
            dma((19,)),
            dma((8, 6)),
            dma((8,)),
            dma((8,)),
            dma((n_z,)),
            dma((n_z,)),
            dma((4,)),
            dma((4,)),
            pltpu.SemaphoreType.REGULAR,
            pltpu.SemaphoreType.REGULAR,
        ],
        compiler_params=pltpu.CompilerParams(
            collective_id=0, has_side_effects=True, vmem_limit_bytes=48 * 2**20
        ),
        cost_estimate=pl.CostEstimate(flops=10**10, bytes_accessed=10**7, transcendentals=4 * 10**6),
    )(*(pltpu.with_memory_space_constraint(a, pltpu.HBM) for a in operands))
    return pl.pallas_call(
        finish,
        out_shape=(
            jax.ShapeDtypeStruct((1,), F32),
            jax.ShapeDtypeStruct((nq, width), F32),
            jax.ShapeDtypeStruct((np_, width), F32),
        ),
        in_specs=[inside] * 3,
        out_specs=(inside, anywhere, anywhere),
        scratch_shapes=[dma((2,))],
        compiler_params=pltpu.CompilerParams(vmem_limit_bytes=4 * 2**20),
    )(loss, gq, gp)


def solution(mesh):
    whole = P(("rep", "row", "col"), None)
    return jax.shard_map(
        functools.partial(local, mesh.shape["row"], mesh.shape["col"]),
        mesh=mesh,
        in_specs=(whole, whole, P(("rep", "row", "col")), whole, whole),
        out_specs=(P("rep"), whole, whole),
        check_vma=False,
    )
```

```python
import functools

import jax
import jax.numpy as jnp
from jax import lax
from jax.experimental import pallas as pl
from jax.experimental.pallas import tpu as pltpu
from jax.sharding import PartitionSpec as P

MESH = pl.DeviceIdType.MESH
BLK = 128
LOWEST = -1e30
F32, BF16, I32 = jnp.float32, jnp.bfloat16, jnp.int32

OWN, SIB, FRONT, BACK, FAR, Y1, Y2, Y3 = range(8)
SEEN_AS = {SIB: SIB, FRONT: BACK, BACK: FRONT, FAR: FAR, Y1: Y3, Y2: Y2, Y3: Y1}


def nt(a, b):
    return lax.dot_general(a, b, (((1,), (1,)), ((), ())), preferred_element_type=F32)


def tn(a, b):
    return lax.dot_general(a, b, (((0,), (0,)), ((), ())), preferred_element_type=F32)


def kernel(
    n_row, n_col, n_z,
    q_hbm, p_hbm, pos_hbm, bm_hbm, ro_hbm,
    loss_ref, gq_ref, gp_ref,
    q, pall, qr, pos, bm, ro, vis, ebuf, wbuf, mrow, run_m, run_l, lt, psc, meta_out, meta_in, zin, xin,
    loc_s, p_ss, p_rs, q_ss, q_rs, m_ss, m_rs, z_ss, z_rs, x_ss, x_rs, y_in, z_in,
):
    nq, width = q.shape
    np_ = pall.shape[1]
    blocks = np_ // BLK
    scale = width ** (-0.5)
    hq, hp = nq // 2, np_ // 2
    r, c = lax.axis_index("row"), lax.axis_index("col")
    odd = lax.rem(r, 2)
    s = 1 - 2 * odd

    def at_row(o):
        return {"row": lax.rem(r + o + n_row, n_row), "col": c}

    def at_col(o):
        return {"row": r, "col": lax.rem(c + o + n_col, n_col)}

    where = {
        SIB: at_row(s), FRONT: at_row(2 * s), BACK: at_row(-2 * s), FAR: at_row(-s),
        Y1: at_col(-1), Y2: at_col(-2), Y3: at_col(1),
    }
    z = lax.rem(lax.div(r, 2), n_z)
    side = lax.div(r, 2 * n_z)
    along_z = {i: {"row": side * 2 * n_z + 2 * lax.rem(z + i, n_z) + odd, "col": c} for i in range(1, n_z)}
    over_x = (1 - side) * 2 * n_z + 2 * z
    same_z = {1: where[SIB], 2: {"row": over_x + odd, "col": c}, 3: {"row": over_x + 1 - odd, "col": c}}

    barrier = pltpu.get_barrier_semaphore()
    chip = r - odd
    even_core, odd_core = {"row": chip, "col": c}, {"row": chip + 1, "col": c}
    for o in range(1, n_col):
        pl.semaphore_signal(
            barrier, inc=1, device_id={"row": chip, "col": lax.rem(c + o, n_col)}, device_id_type=MESH
        )

    @pl.when(odd == 1)
    def _():
        pl.semaphore_signal(barrier, inc=1, device_id=even_core, device_id_type=MESH)

    loads = [
        pltpu.make_async_copy(src, dst, loc_s.at[i])
        for i, (src, dst) in enumerate(
            ((q_hbm, q), (p_hbm, pall.at[OWN]), (bm_hbm, bm), (ro_hbm, ro), (pos_hbm, pos))
        )
    ]

    @pl.when(odd == 0)
    def _():
        pl.semaphore_wait(barrier, 2 * (n_col - 1) + 1)
        pl.semaphore_signal(y_in, inc=1, device_id=odd_core, device_id_type=MESH)

    @pl.when(odd == 1)
    def _():
        pl.semaphore_wait(y_in, 1)

    class Sender:
        def __init__(self, ss, rs, land):
            self.ss, self.rs, self.land, self.n, self.sent = ss, rs, land, 0, []

        def __call__(self, src, slot, to, first, rows, mark):
            cp = pltpu.make_async_remote_copy(
                src_ref=src.at[pl.ds(first, rows)],
                dst_ref=self.land(slot).at[pl.ds(first, rows)],
                send_sem=self.ss.at[self.n],
                recv_sem=self.rs.at[slot, mark],
                device_id=where[to],
                device_id_type=MESH,
            )
            self.n += 1
            self.sent.append(cp)
            cp.start()
            return cp

    send_p = Sender(p_ss, p_rs, lambda k: pall.at[k])
    send_q = Sender(q_ss, q_rs, lambda k: qr.at[k - 1])

    pa0 = send_p(p_hbm, Y1, Y3, 0, hp, 0)
    pb1 = send_p(p_hbm, Y3, Y1, hp, hp, 1)
    pa1 = send_p(p_hbm, Y1, Y3, hp, hp, 1)
    pb0 = send_p(p_hbm, Y3, Y1, 0, hp, 0)
    for cp in loads:
        cp.start()
    p_sib = send_p(p_hbm, SIB, SIB, 0, np_, 0)
    q_sib = send_q(q_hbm, SIB, SIB, 0, nq, 0)

    chips = [lax.rem(chip + 2, n_row), lax.rem(chip + n_row - 2, n_row), over_x]
    chips += [to["row"] - odd for to in along_z.values()]
    for there in chips:
        pl.semaphore_signal(barrier, inc=1, device_id={"row": there + 1, "col": c}, device_id_type=MESH)

    @pl.when(odd == 1)
    def _():
        pl.semaphore_wait(barrier, 2 * len(chips))
        pl.semaphore_signal(z_in, inc=1, device_id=even_core, device_id_type=MESH)

    @pl.when(odd == 0)
    def _():
        pl.semaphore_wait(z_in, 1)

    p_front = send_p(p_hbm, BACK, FRONT, 0, np_, 0)
    p_back = send_p(p_hbm, FRONT, BACK, 0, np_, 0)
    qz = nq * 5 // 8
    q_front = [send_q(q_hbm, BACK, FRONT, 0, qz, 0)]
    q_back = [send_q(q_hbm, FRONT, BACK, 0, qz, 0)]

    for cp in loads:
        cp.wait()
    row_i = lax.broadcasted_iota(I32, (64, 1), 0)
    slot_i, block_i = lax.shift_right_logical(row_i, 3), lax.bitwise_and(row_i, 7)
    up = jnp.where(odd == 0, jnp.int32(1), jnp.int32(0))
    group = jnp.where(
        slot_i == SIB, 2 + up,
        jnp.where(slot_i == FRONT, 1 + 3 * up, jnp.where(slot_i == BACK, 4 - 3 * up, jnp.where(slot_i == FAR, 3 - up, 0))),
    )
    nb = bm.shape[0]
    wanted = jnp.where((slot_i <= FAR) & (block_i < blocks), group * blocks + block_i, -1)
    pick = jnp.where(lax.broadcasted_iota(I32, (64, nb), 1) == wanted, 1.0, 0.0).astype(BF16)
    seen = jnp.dot(pick, bm[...].astype(F32).astype(BF16), preferred_element_type=F32)
    nr = ro.shape[0]
    pick_r = jnp.where(lax.broadcasted_iota(I32, (64, nr), 1) == slot_i - Y1, 1.0, 0.0).astype(BF16)
    listed = jnp.dot(pick_r, ro[...].astype(F32).astype(BF16), preferred_element_type=F32)
    in_roster = jnp.where(jnp.abs(listed - block_i.astype(F32)) < 0.5, 1.0, 0.0)
    seen = jnp.where(slot_i >= Y1, in_roster, seen)
    pos_row = pos[...]
    own_block = jnp.where((slot_i == OWN) & (lax.shift_right_logical(pos_row, 7) == block_i), 1.0, 0.0)
    seen = jnp.maximum(seen, own_block)
    for k in range(8):
        vis[k] = seen[8 * k : 8 * k + 8]

    run_m[...] = jnp.full(run_m.shape, LOWEST, F32)
    run_l[...] = jnp.zeros(run_l.shape, F32)

    def forward(k):
        @pl.loop(0, 2)
        def _(h):
            cols = pl.ds(pl.multiple_of(h * hq, hq), hq)
            sc = nt(pall[k], q[cols, :]) * scale
            v = vis[k, :, cols]
            m_old = run_m[0:1, cols]
            m_new = m_old
            for b in range(blocks):
                top = jnp.max(sc[b * BLK : (b + 1) * BLK], axis=0, keepdims=True)
                m_new = jnp.maximum(m_new, jnp.where(v[b : b + 1] > 0.5, top, LOWEST))
            total = run_l[0:1, cols] * jnp.exp(m_old - m_new)
            for b in range(blocks):
                bias = jnp.where(v[b : b + 1] > 0.5, -m_new, LOWEST)
                e = jnp.exp(sc[b * BLK : (b + 1) * BLK] + bias)
                total = total + jnp.sum(e, axis=0, keepdims=True)
                ebuf[k, b * BLK : (b + 1) * BLK, cols] = e
            if k == OWN:
                target = lax.broadcasted_iota(I32, (np_, hq), 0) == pos[0:1, cols]
                psc[0:1, cols] = jnp.sum(jnp.where(target, sc, 0.0), axis=0, keepdims=True)
            run_m[0:1, cols] = m_new
            run_l[0:1, cols] = total
            mrow[k, 0:1, cols] = m_new

    forward(OWN)
    p_sib.wait_recv()
    forward(SIB)
    pa0.wait_recv()
    ra = send_p(pall.at[Y1], Y2, Y3, 0, hp, 0)
    pb1.wait_recv()
    rb = send_p(pall.at[Y3], Y2, Y1, hp, hp, 1)
    pa1.wait_recv()
    pb0.wait_recv()
    q0 = nq * 3 // 8
    qa = [send_q(q_hbm, Y1, Y3, 0, q0, 0), send_q(q_hbm, Y1, Y3, q0, hq - q0, 1)]
    qb = [send_q(q_hbm, Y3, Y1, nq - q0, q0, 0), send_q(q_hbm, Y3, Y1, hq, hq - q0, 1)]
    forward(Y1)
    forward(Y3)
    p_back.wait_recv()
    p_far = send_p(pall.at[FRONT], FAR, SIB, 0, np_, 0)
    p_front.wait_recv()
    forward(FRONT)
    forward(BACK)
    p_far.wait_recv()
    forward(FAR)
    ra.wait_recv()
    rb.wait_recv()
    forward(Y2)

    lt[0:1] = run_m[0:1] + jnp.log(run_l[0:1])
    own_loss = jnp.sum(lt[0:1] - psc[0:1], axis=1, keepdims=True)
    metas = {}
    for k in (Y1, Y3, Y2, FRONT, BACK, FAR, SIB):
        rows = jnp.where(vis[k] > 0.5, -lt[0:1], LOWEST)
        last = lax.broadcasted_iota(I32, rows.shape, 0) == 7
        meta_out[k] = jnp.where(last, own_loss, rows)
        seen_as = SEEN_AS[k]
        cp = pltpu.make_async_remote_copy(
            src_ref=meta_out.at[k], dst_ref=meta_in.at[seen_as],
            send_sem=m_ss.at[k], recv_sem=m_rs.at[seen_as],
            device_id=where[k], device_id_type=MESH,
        )
        cp.start()
        metas[seen_as] = cp
    q_front.append(send_q(q_hbm, BACK, FRONT, qz, nq - qz, 1))
    q_back.append(send_q(q_hbm, FRONT, BACK, qz, nq - qz, 1))
    qa.append(send_q(q_hbm, Y1, Y3, hq, hq, 2))
    qb.append(send_q(q_hbm, Y3, Y1, 0, hq, 2))

    for k in range(8):
        @pl.loop(0, 2)
        def _(h):
            cols = pl.ds(pl.multiple_of(h * hq, hq), hq)
            factor = jnp.exp(mrow[k, 0:1, cols] - lt[0:1, cols])
            w = ebuf[k, :, cols] * factor
            if k == OWN:
                target = lax.broadcasted_iota(I32, (np_, hq), 0) == pos[0:1, cols]
                w = w - jnp.where(target, 1.0, 0.0)
            wbuf[k * np_ : (k + 1) * np_, cols] = w.astype(BF16)

    gp_ref[...] = jnp.dot(wbuf[0:np_, :], q[...], preferred_element_type=F32) * scale

    def own_gradient(first):
        cols = pl.ds(first, hq)
        total = tn(wbuf[0:np_, cols], pall[0])
        for k in range(1, 8):
            total = total + tn(wbuf[k * np_ : (k + 1) * np_, cols], pall[k])
        gq_ref[cols, :] = total * scale

    own_gradient(0)

    def backward(k, first, rows):
        span = pl.ds(first, rows)
        sc = nt(pall[OWN], qr[k - 1, span, :]) * scale
        parts = []
        for b in range(blocks):
            parts.append(jnp.exp(sc[b * BLK : (b + 1) * BLK] + meta_in[k, b : b + 1, span]).astype(BF16))
        w = jnp.concatenate(parts, axis=0)
        gp_ref[...] += jnp.dot(w, qr[k - 1, span, :], preferred_element_type=F32) * scale

    loss_at = lambda k: meta_in[k, 7:8, 0:128]
    for k in (Y1, Y3, Y2):
        metas[k].wait_recv()
    near = loss_at(Y1) + loss_at(Y3)
    mine = meta_out[Y1, 7:8, 0:128] + loss_at(Y2)
    zin[0] = jnp.broadcast_to(near + mine, (8, 128))

    def spread(buf, ss, rs, partners):
        copies = []
        for i, to in partners.items():
            cp = pltpu.make_async_remote_copy(
                src_ref=buf.at[0], dst_ref=buf.at[i], send_sem=ss.at[i], recv_sem=rs.at[i],
                device_id=to, device_id_type=MESH,
            )
            cp.start()
            copies.append(cp)
        return copies

    loss_z = spread(zin, z_ss, z_rs, along_z)

    qa[0].wait_recv()
    ra2 = [send_q(qr.at[Y1 - 1], Y2, Y3, 0, q0, 0)]
    qb[0].wait_recv()
    rb2 = [send_q(qr.at[Y3 - 1], Y2, Y1, nq - q0, q0, 2)]
    own_gradient(hq)
    qa[1].wait_recv()
    ra2.append(send_q(qr.at[Y1 - 1], Y2, Y3, q0, hq - q0, 1))
    qb[1].wait_recv()
    rb2.append(send_q(qr.at[Y3 - 1], Y2, Y1, hq, hq - q0, 3))
    metas[SIB].wait_recv()
    q_sib.wait_recv()
    backward(SIB, 0, hq)
    backward(SIB, hq, hq)
    backward(Y1, 0, hq)
    backward(Y3, hq, hq)
    q_back[0].wait_recv()
    q_far = [send_q(qr.at[FRONT - 1], FAR, SIB, 0, qz, 0)]
    metas[FRONT].wait_recv()
    backward(FRONT, 0, hq)
    metas[BACK].wait_recv()
    q_front[0].wait_recv()
    backward(BACK, 0, hq)
    metas[FAR].wait_recv()
    q_far[0].wait_recv()
    backward(FAR, 0, hq)
    for cp in loss_z:
        cp.wait_recv()
    total = zin[z]
    for i in range(1, n_z):
        total = total + zin[lax.rem(z + n_z - i, n_z)]
    xin[0] = total
    loss_x = spread(xin, x_ss, x_rs, same_z)
    q_back[1].wait_recv()
    q_far.append(send_q(qr.at[FRONT - 1], FAR, SIB, qz, nq - qz, 1))
    backward(FRONT, hq, hq)
    q_front[1].wait_recv()
    backward(BACK, hq, hq)
    qa[2].wait_recv()
    backward(Y1, hq, hq)
    qb[2].wait_recv()
    backward(Y3, 0, hq)
    q_far[1].wait_recv()
    backward(FAR, hq, hq)
    for cp in loss_x:
        cp.wait_recv()
    loss_ref[...] = ((xin[0] + xin[1]) + (xin[2] + xin[3])) * (1.0 / (nq * n_row * n_col))
    ra2[0].wait_recv()
    backward(Y2, 0, q0)
    rb2[0].wait_recv()
    backward(Y2, nq - q0, q0)
    ra2[1].wait_recv()
    rb2[1].wait_recv()
    backward(Y2, q0, nq - 2 * q0)

    for cp in send_p.sent + send_q.sent + list(metas.values()) + loss_z + loss_x:
        cp.wait_send()


def finish(loss, gq, gp, loss_out, gq_out, gp_out, sems):
    copies = [pltpu.make_async_copy(gq, gq_out, sems.at[0]), pltpu.make_async_copy(gp, gp_out, sems.at[1]), pltpu.make_async_copy(loss.at[pl.ds(0, 1)], loss_out, sems.at[2])]
    for cp in copies:
        cp.start()
    for cp in copies:
        cp.wait()


def local(n_row, n_col, queries, passages, positive, block_mask, roster):
    nq, width = queries.shape
    np_ = passages.shape[0]
    n_z = n_row // 4
    nb, nr = block_mask.shape[1], roster.shape[1]
    anywhere = pl.BlockSpec(memory_space=pltpu.HBM)
    inside = pl.BlockSpec(memory_space=pltpu.VMEM)
    dma = pltpu.SemaphoreType.DMA
    operands = (queries, passages, positive.reshape(1, nq), block_mask.T, roster.T)
    loss, gq, gp = pl.pallas_call(
        functools.partial(kernel, n_row, n_col, n_z),
        out_shape=(
            jax.ShapeDtypeStruct((8, 128), F32),
            jax.ShapeDtypeStruct((nq, width), F32),
            jax.ShapeDtypeStruct((np_, width), F32),
        ),
        in_specs=[anywhere] * 5,
        out_specs=(inside,) * 3,
        scratch_shapes=[
            pltpu.VMEM((nq, width), BF16),
            pltpu.VMEM((8, np_, width), BF16),
            pltpu.VMEM((7, nq, width), BF16),
            pltpu.VMEM((1, nq), I32),
            pltpu.VMEM((nb, nq), I32),
            pltpu.VMEM((nr, nq), I32),
            pltpu.VMEM((8, 8, nq), F32),
            pltpu.VMEM((8, np_, nq), F32),
            pltpu.VMEM((8 * np_, nq), BF16),
            pltpu.VMEM((8, 8, nq), F32),
            pltpu.VMEM((8, nq), F32),
            pltpu.VMEM((8, nq), F32),
            pltpu.VMEM((8, nq), F32),
            pltpu.VMEM((8, nq), F32),
            pltpu.VMEM((8, 8, nq), F32),
            pltpu.VMEM((8, 8, nq), F32),
            pltpu.VMEM((n_z, 8, 128), F32),
            pltpu.VMEM((4, 8, 128), F32),
            dma((5,)),
            dma((10,)),
            dma((8, 2)),
            dma((17,)),
            dma((8, 4)),
            dma((8,)),
            dma((8,)),
            dma((n_z,)),
            dma((n_z,)),
            dma((4,)),
            dma((4,)),
            pltpu.SemaphoreType.REGULAR,
            pltpu.SemaphoreType.REGULAR,
        ],
        compiler_params=pltpu.CompilerParams(
            collective_id=0, has_side_effects=True, vmem_limit_bytes=48 * 2**20
        ),
        cost_estimate=pl.CostEstimate(flops=10**10, bytes_accessed=10**7, transcendentals=4 * 10**6),
    )(*(pltpu.with_memory_space_constraint(a, pltpu.HBM) for a in operands))
    a, b, d = pl.pallas_call(
        finish,
        out_shape=(
            jax.ShapeDtypeStruct((1, 128), F32),
            jax.ShapeDtypeStruct((nq, width), F32),
            jax.ShapeDtypeStruct((np_, width), F32),
        ),
        in_specs=[inside] * 3,
        out_specs=(anywhere, anywhere, anywhere),
        scratch_shapes=[dma((3,))],
        compiler_params=pltpu.CompilerParams(vmem_limit_bytes=4 * 2**20),
    )(loss, gq, gp)
    return a[0, 0:1], b, d


def solution(mesh):
    whole = P(("rep", "row", "col"), None)
    return jax.shard_map(
        functools.partial(local, mesh.shape["row"], mesh.shape["col"]),
        mesh=mesh,
        in_specs=(whole, whole, P(("rep", "row", "col")), whole, whole),
        out_specs=(P("rep"), whole, whole),
        check_vma=False,
    )
```

```python
import functools

import jax
import jax.numpy as jnp
from jax import lax
from jax.experimental import pallas as pl
from jax.experimental.pallas import tpu as pltpu
from jax.sharding import PartitionSpec as P

MESH = pl.DeviceIdType.MESH
BLK = 128
LOWEST = -1e30
F32, BF16, I32 = jnp.float32, jnp.bfloat16, jnp.int32

OWN, SIB, FRONT, BACK, FAR, Y1, Y2, Y3 = range(8)
SEEN_AS = {SIB: SIB, FRONT: BACK, BACK: FRONT, FAR: FAR, Y1: Y3, Y2: Y2, Y3: Y1}


def nt(a, b):
    return lax.dot_general(a, b, (((1,), (1,)), ((), ())), preferred_element_type=F32)


def tn(a, b):
    return lax.dot_general(a, b, (((0,), (0,)), ((), ())), preferred_element_type=F32)


def kernel(
    n_row, n_col, n_z,
    q_hbm, p_hbm, pos_hbm, bm_hbm, ro_hbm,
    loss_ref, gq_ref, gp_ref, p_own, q_tail, m_tail,
    q, pall, qr, pos, bm, ro, vis, ebuf, wbuf, mrow, run_m, run_l, lt, psc, meta_out, meta_in, zin, xin,
    loc_s, p_ss, p_rs, q_ss, q_rs, m_ss, m_rs, z_ss, z_rs, x_ss, x_rs, y_in, z_in,
):
    nq, width = q.shape
    np_ = pall.shape[1]
    blocks = np_ // BLK
    scale = width ** (-0.5)
    hq, hp = nq // 2, np_ // 2
    r, c = lax.axis_index("row"), lax.axis_index("col")
    odd = lax.rem(r, 2)
    s = 1 - 2 * odd

    def at_row(o):
        return {"row": lax.rem(r + o + n_row, n_row), "col": c}

    def at_col(o):
        return {"row": r, "col": lax.rem(c + o + n_col, n_col)}

    where = {
        SIB: at_row(s), FRONT: at_row(2 * s), BACK: at_row(-2 * s), FAR: at_row(-s),
        Y1: at_col(-1), Y2: at_col(-2), Y3: at_col(1),
    }
    z = lax.rem(lax.div(r, 2), n_z)
    side = lax.div(r, 2 * n_z)
    along_z = {i: {"row": side * 2 * n_z + 2 * lax.rem(z + i, n_z) + odd, "col": c} for i in range(1, n_z)}
    over_x = (1 - side) * 2 * n_z + 2 * z
    same_z = {1: where[SIB], 2: {"row": over_x + odd, "col": c}, 3: {"row": over_x + 1 - odd, "col": c}}

    barrier = pltpu.get_barrier_semaphore()
    chip = r - odd
    even_core, odd_core = {"row": chip, "col": c}, {"row": chip + 1, "col": c}
    for o in range(1, n_col):
        pl.semaphore_signal(
            barrier, inc=1, device_id={"row": chip, "col": lax.rem(c + o, n_col)}, device_id_type=MESH
        )

    @pl.when(odd == 1)
    def _():
        pl.semaphore_signal(barrier, inc=1, device_id=even_core, device_id_type=MESH)

    loads = [
        pltpu.make_async_copy(src, dst, loc_s.at[i])
        for i, (src, dst) in enumerate(
            ((q_hbm, q), (p_hbm, pall.at[OWN]), (bm_hbm, bm), (ro_hbm, ro), (pos_hbm, pos))
        )
    ]

    @pl.when(odd == 0)
    def _():
        pl.semaphore_wait(barrier, 2 * (n_col - 1) + 1)
        pl.semaphore_signal(y_in, inc=1, device_id=odd_core, device_id_type=MESH)

    @pl.when(odd == 1)
    def _():
        pl.semaphore_wait(y_in, 1)

    class Sender:
        def __init__(self, ss, rs, land):
            self.ss, self.rs, self.land, self.n, self.sent = ss, rs, land, 0, []

        def __call__(self, src, slot, to, first, rows, mark):
            cp = pltpu.make_async_remote_copy(
                src_ref=src.at[pl.ds(first, rows)],
                dst_ref=self.land(slot).at[pl.ds(first, rows)],
                send_sem=self.ss.at[self.n],
                recv_sem=self.rs.at[slot, mark],
                device_id=where[to],
                device_id_type=MESH,
            )
            self.n += 1
            self.sent.append(cp)
            cp.start()
            return cp

    send_p = Sender(p_ss, p_rs, lambda k: pall.at[k])
    send_q = Sender(q_ss, q_rs, lambda k: qr.at[k - 1])

    pa0 = send_p(p_hbm, Y1, Y3, 0, hp, 0)
    pb1 = send_p(p_hbm, Y3, Y1, hp, hp, 1)
    pa1 = send_p(p_hbm, Y1, Y3, hp, hp, 1)
    pb0 = send_p(p_hbm, Y3, Y1, 0, hp, 0)
    for cp in loads:
        cp.start()
    p_sib = send_p(p_hbm, SIB, SIB, 0, np_, 0)
    q_sib = send_q(q_hbm, SIB, SIB, 0, nq, 0)

    chips = [lax.rem(chip + 2, n_row), lax.rem(chip + n_row - 2, n_row), over_x]
    chips += [to["row"] - odd for to in along_z.values()]
    for there in chips:
        pl.semaphore_signal(barrier, inc=1, device_id={"row": there + 1, "col": c}, device_id_type=MESH)

    @pl.when(odd == 1)
    def _():
        pl.semaphore_wait(barrier, 2 * len(chips))
        pl.semaphore_signal(z_in, inc=1, device_id=even_core, device_id_type=MESH)

    @pl.when(odd == 0)
    def _():
        pl.semaphore_wait(z_in, 1)

    p_front = send_p(p_hbm, BACK, FRONT, 0, np_, 0)
    p_back = send_p(p_hbm, FRONT, BACK, 0, np_, 0)
    qz = nq * 5 // 8
    q_front = [send_q(q_hbm, BACK, FRONT, 0, qz, 0)]
    q_back = [send_q(q_hbm, FRONT, BACK, 0, qz, 0)]

    for cp in loads:
        cp.wait()
    row_i = lax.broadcasted_iota(I32, (64, 1), 0)
    slot_i, block_i = lax.shift_right_logical(row_i, 3), lax.bitwise_and(row_i, 7)
    up = jnp.where(odd == 0, jnp.int32(1), jnp.int32(0))
    group = jnp.where(
        slot_i == SIB, 2 + up,
        jnp.where(slot_i == FRONT, 1 + 3 * up, jnp.where(slot_i == BACK, 4 - 3 * up, jnp.where(slot_i == FAR, 3 - up, 0))),
    )
    nb = bm.shape[0]
    wanted = jnp.where((slot_i <= FAR) & (block_i < blocks), group * blocks + block_i, -1)
    pick = jnp.where(lax.broadcasted_iota(I32, (64, nb), 1) == wanted, 1.0, 0.0).astype(BF16)
    seen = jnp.dot(pick, bm[...].astype(F32).astype(BF16), preferred_element_type=F32)
    nr = ro.shape[0]
    pick_r = jnp.where(lax.broadcasted_iota(I32, (64, nr), 1) == slot_i - Y1, 1.0, 0.0).astype(BF16)
    listed = jnp.dot(pick_r, ro[...].astype(F32).astype(BF16), preferred_element_type=F32)
    in_roster = jnp.where(jnp.abs(listed - block_i.astype(F32)) < 0.5, 1.0, 0.0)
    seen = jnp.where(slot_i >= Y1, in_roster, seen)
    pos_row = pos[...]
    own_block = jnp.where((slot_i == OWN) & (lax.shift_right_logical(pos_row, 7) == block_i), 1.0, 0.0)
    seen = jnp.maximum(seen, own_block)
    for k in range(8):
        vis[k] = seen[8 * k : 8 * k + 8]

    run_m[...] = jnp.full(run_m.shape, LOWEST, F32)
    run_l[...] = jnp.zeros(run_l.shape, F32)

    def forward(k):
        @pl.loop(0, 2)
        def _(h):
            cols = pl.ds(pl.multiple_of(h * hq, hq), hq)
            sc = nt(pall[k], q[cols, :]) * scale
            v = vis[k, :, cols]
            m_old = run_m[0:1, cols]
            m_new = m_old
            for b in range(blocks):
                top = jnp.max(sc[b * BLK : (b + 1) * BLK], axis=0, keepdims=True)
                m_new = jnp.maximum(m_new, jnp.where(v[b : b + 1] > 0.5, top, LOWEST))
            total = run_l[0:1, cols] * jnp.exp(m_old - m_new)
            for b in range(blocks):
                bias = jnp.where(v[b : b + 1] > 0.5, -m_new, LOWEST)
                e = jnp.exp(sc[b * BLK : (b + 1) * BLK] + bias)
                total = total + jnp.sum(e, axis=0, keepdims=True)
                ebuf[k, b * BLK : (b + 1) * BLK, cols] = e
            if k == OWN:
                target = lax.broadcasted_iota(I32, (np_, hq), 0) == pos[0:1, cols]
                psc[0:1, cols] = jnp.sum(jnp.where(target, sc, 0.0), axis=0, keepdims=True)
            run_m[0:1, cols] = m_new
            run_l[0:1, cols] = total
            mrow[k, 0:1, cols] = m_new

    p_own[...] = pall[OWN]
    forward(OWN)
    p_sib.wait_recv()
    forward(SIB)
    pa0.wait_recv()
    ra = send_p(pall.at[Y1], Y2, Y3, 0, hp, 0)
    pb1.wait_recv()
    rb = send_p(pall.at[Y3], Y2, Y1, hp, hp, 1)
    pa1.wait_recv()
    pb0.wait_recv()
    q0 = nq * 3 // 8
    qa = [send_q(q_hbm, Y1, Y3, 0, q0, 0), send_q(q_hbm, Y1, Y3, q0, hq - q0, 1)]
    qb = [send_q(q_hbm, Y3, Y1, nq - q0, q0, 0), send_q(q_hbm, Y3, Y1, hq, hq - q0, 1)]
    forward(Y1)
    forward(Y3)
    p_back.wait_recv()
    p_far = send_p(pall.at[FRONT], FAR, SIB, 0, np_, 0)
    p_front.wait_recv()
    forward(FRONT)
    forward(BACK)
    p_far.wait_recv()
    forward(FAR)
    ra.wait_recv()
    rb.wait_recv()
    forward(Y2)

    lt[0:1] = run_m[0:1] + jnp.log(run_l[0:1])
    own_loss = jnp.sum(lt[0:1] - psc[0:1], axis=1, keepdims=True)
    metas = {}
    for k in (Y1, Y3, Y2, FRONT, BACK, FAR, SIB):
        rows = jnp.where(vis[k] > 0.5, -lt[0:1], LOWEST)
        last = lax.broadcasted_iota(I32, rows.shape, 0) == 7
        meta_out[k] = jnp.where(last, own_loss, rows)
        seen_as = SEEN_AS[k]
        cp = pltpu.make_async_remote_copy(
            src_ref=meta_out.at[k], dst_ref=meta_in.at[seen_as],
            send_sem=m_ss.at[k], recv_sem=m_rs.at[seen_as],
            device_id=where[k], device_id_type=MESH,
        )
        cp.start()
        metas[seen_as] = cp
    q_front.append(send_q(q_hbm, BACK, FRONT, qz, nq - qz, 1))
    q_back.append(send_q(q_hbm, FRONT, BACK, qz, nq - qz, 1))
    qa.append(send_q(q_hbm, Y1, Y3, hq, hq, 2))
    qb.append(send_q(q_hbm, Y3, Y1, 0, hq, 2))

    for k in range(8):
        @pl.loop(0, 2)
        def _(h):
            cols = pl.ds(pl.multiple_of(h * hq, hq), hq)
            factor = jnp.exp(mrow[k, 0:1, cols] - lt[0:1, cols])
            w = ebuf[k, :, cols] * factor
            if k == OWN:
                target = lax.broadcasted_iota(I32, (np_, hq), 0) == pos[0:1, cols]
                w = w - jnp.where(target, 1.0, 0.0)
            wbuf[k * np_ : (k + 1) * np_, cols] = w.astype(BF16)

    gp_ref[...] = jnp.dot(wbuf[0:np_, :], q[...], preferred_element_type=F32) * scale

    def own_gradient(first):
        cols = pl.ds(first, hq)
        total = tn(wbuf[0:np_, cols], pall[0])
        for k in range(1, 8):
            total = total + tn(wbuf[k * np_ : (k + 1) * np_, cols], pall[k])
        gq_ref[cols, :] = total * scale

    own_gradient(0)

    def backward(k, first, rows):
        span = pl.ds(first, rows)
        sc = nt(pall[OWN], qr[k - 1, span, :]) * scale
        parts = []
        for b in range(blocks):
            parts.append(jnp.exp(sc[b * BLK : (b + 1) * BLK] + meta_in[k, b : b + 1, span]).astype(BF16))
        w = jnp.concatenate(parts, axis=0)
        gp_ref[...] += jnp.dot(w, qr[k - 1, span, :], preferred_element_type=F32) * scale

    loss_at = lambda k: meta_in[k, 7:8, 0:128]
    for k in (Y1, Y3, Y2):
        metas[k].wait_recv()
    near = loss_at(Y1) + loss_at(Y3)
    mine = meta_out[Y1, 7:8, 0:128] + loss_at(Y2)
    zin[0] = jnp.broadcast_to(near + mine, (8, 128))

    def spread(buf, ss, rs, partners):
        copies = []
        for i, to in partners.items():
            cp = pltpu.make_async_remote_copy(
                src_ref=buf.at[0], dst_ref=buf.at[i], send_sem=ss.at[i], recv_sem=rs.at[i],
                device_id=to, device_id_type=MESH,
            )
            cp.start()
            copies.append(cp)
        return copies

    loss_z = spread(zin, z_ss, z_rs, along_z)

    qa[0].wait_recv()
    ra2 = [send_q(qr.at[Y1 - 1], Y2, Y3, 0, q0, 0)]
    qb[0].wait_recv()
    rb2 = [send_q(qr.at[Y3 - 1], Y2, Y1, nq - q0, q0, 2)]
    own_gradient(hq)
    qa[1].wait_recv()
    ra2.append(send_q(qr.at[Y1 - 1], Y2, Y3, q0, hq - q0, 1))
    qb[1].wait_recv()
    rb2.append(send_q(qr.at[Y3 - 1], Y2, Y1, hq, hq - q0, 3))
    metas[SIB].wait_recv()
    q_sib.wait_recv()
    backward(SIB, 0, hq)
    backward(SIB, hq, hq)
    backward(Y1, 0, hq)
    backward(Y3, hq, hq)
    q_back[0].wait_recv()
    q_far = [send_q(qr.at[FRONT - 1], FAR, SIB, 0, qz, 0)]
    metas[FRONT].wait_recv()
    backward(FRONT, 0, hq)
    metas[BACK].wait_recv()
    q_front[0].wait_recv()
    backward(BACK, 0, hq)
    metas[FAR].wait_recv()
    q_far[0].wait_recv()
    backward(FAR, 0, hq)
    for cp in loss_z:
        cp.wait_recv()
    total = zin[z]
    for i in range(1, n_z):
        total = total + zin[lax.rem(z + n_z - i, n_z)]
    xin[0] = total
    loss_x = spread(xin, x_ss, x_rs, same_z)
    q_back[1].wait_recv()
    q_far.append(send_q(qr.at[FRONT - 1], FAR, SIB, qz, nq - qz, 1))
    backward(FRONT, hq, hq)
    q_front[1].wait_recv()
    backward(BACK, hq, hq)
    qa[2].wait_recv()
    backward(Y1, hq, hq)
    qb[2].wait_recv()
    backward(Y3, 0, hq)
    q_far[1].wait_recv()
    backward(FAR, hq, hq)
    for cp in loss_x:
        cp.wait_recv()
    loss_ref[...] = ((xin[0] + xin[1]) + (xin[2] + xin[3])) * (1.0 / (nq * n_row * n_col))
    m_tail[...] = meta_in[Y2, :, q0 : nq - q0]
    ra2[0].wait_recv()
    backward(Y2, 0, q0)
    rb2[0].wait_recv()
    backward(Y2, nq - q0, q0)
    ra2[1].wait_recv()
    rb2[1].wait_recv()
    q_tail[...] = qr[Y2 - 1, q0 : nq - q0, :]

    for cp in send_p.sent + send_q.sent + list(metas.values()) + loss_z + loss_x:
        cp.wait_send()


def finish(loss, gq, gp, p_own, q_tail, m_tail, loss_out, gq_out, gp_out, gp_sum, sems):
    copies = [
        pltpu.make_async_copy(gq, gq_out, sems.at[0]),
        pltpu.make_async_copy(loss.at[pl.ds(0, 1)], loss_out, sems.at[1]),
    ]
    for cp in copies:
        cp.start()
    scale = gq.shape[1] ** (-0.5)
    for b in range(gp.shape[0] // BLK):
        rows = pl.ds(b * BLK, BLK)
        w = jnp.exp(nt(p_own[rows, :], q_tail[...]) * scale + m_tail[b : b + 1, :]).astype(BF16)
        gp_sum[rows, :] = gp[rows, :] + jnp.dot(w, q_tail[...], preferred_element_type=F32) * scale
        copies.append(pltpu.make_async_copy(gp_sum.at[rows], gp_out.at[rows], sems.at[2 + b]))
        copies[-1].start()
    for cp in copies:
        cp.wait()


def local(n_row, n_col, queries, passages, positive, block_mask, roster):
    nq, width = queries.shape
    np_ = passages.shape[0]
    n_z = n_row // 4
    nb, nr = block_mask.shape[1], roster.shape[1]
    anywhere = pl.BlockSpec(memory_space=pltpu.HBM)
    inside = pl.BlockSpec(memory_space=pltpu.VMEM)
    dma = pltpu.SemaphoreType.DMA
    operands = (queries, passages, positive.reshape(1, nq), block_mask.T, roster.T)
    loss, gq, *rest = pl.pallas_call(
        functools.partial(kernel, n_row, n_col, n_z),
        out_shape=(
            jax.ShapeDtypeStruct((8, 128), F32),
            jax.ShapeDtypeStruct((nq, width), F32),
            jax.ShapeDtypeStruct((np_, width), F32),
            jax.ShapeDtypeStruct((np_, width), BF16),
            jax.ShapeDtypeStruct((nq // 4, width), BF16),
            jax.ShapeDtypeStruct((8, nq // 4), F32),
        ),
        in_specs=[anywhere] * 5,
        out_specs=(inside,) * 6,
        scratch_shapes=[
            pltpu.VMEM((nq, width), BF16),
            pltpu.VMEM((8, np_, width), BF16),
            pltpu.VMEM((7, nq, width), BF16),
            pltpu.VMEM((1, nq), I32),
            pltpu.VMEM((nb, nq), I32),
            pltpu.VMEM((nr, nq), I32),
            pltpu.VMEM((8, 8, nq), F32),
            pltpu.VMEM((8, np_, nq), F32),
            pltpu.VMEM((8 * np_, nq), BF16),
            pltpu.VMEM((8, 8, nq), F32),
            pltpu.VMEM((8, nq), F32),
            pltpu.VMEM((8, nq), F32),
            pltpu.VMEM((8, nq), F32),
            pltpu.VMEM((8, nq), F32),
            pltpu.VMEM((8, 8, nq), F32),
            pltpu.VMEM((8, 8, nq), F32),
            pltpu.VMEM((n_z, 8, 128), F32),
            pltpu.VMEM((4, 8, 128), F32),
            dma((5,)),
            dma((10,)),
            dma((8, 2)),
            dma((17,)),
            dma((8, 4)),
            dma((8,)),
            dma((8,)),
            dma((n_z,)),
            dma((n_z,)),
            dma((4,)),
            dma((4,)),
            pltpu.SemaphoreType.REGULAR,
            pltpu.SemaphoreType.REGULAR,
        ],
        compiler_params=pltpu.CompilerParams(
            collective_id=0, has_side_effects=True, vmem_limit_bytes=48 * 2**20
        ),
        cost_estimate=pl.CostEstimate(flops=10**10, bytes_accessed=10**7, transcendentals=4 * 10**6),
    )(*(pltpu.with_memory_space_constraint(a, pltpu.HBM) for a in operands))
    a, b, d = pl.pallas_call(
        finish,
        out_shape=(
            jax.ShapeDtypeStruct((1, 128), F32),
            jax.ShapeDtypeStruct((nq, width), F32),
            jax.ShapeDtypeStruct((np_, width), F32),
        ),
        in_specs=[inside] * 6,
        out_specs=(anywhere, anywhere, anywhere),
        scratch_shapes=[pltpu.VMEM((np_, width), F32), dma((2 + np_ // BLK,))],
        compiler_params=pltpu.CompilerParams(vmem_limit_bytes=8 * 2**20),
    )(loss, gq, *rest)
    return a[0, 0:1], b, d


def solution(mesh):
    whole = P(("rep", "row", "col"), None)
    return jax.shard_map(
        functools.partial(local, mesh.shape["row"], mesh.shape["col"]),
        mesh=mesh,
        in_specs=(whole, whole, P(("rep", "row", "col")), whole, whole),
        out_specs=(P("rep"), whole, whole),
        check_vma=False,
    )
```

```python
import functools

import jax
import jax.numpy as jnp
from jax import lax
from jax.experimental import pallas as pl
from jax.experimental.pallas import tpu as pltpu
from jax.sharding import PartitionSpec as P

MESH = pl.DeviceIdType.MESH
BLK = 128
LOWEST = -1e30
F32, BF16, I32 = jnp.float32, jnp.bfloat16, jnp.int32

OWN, SIB, FRONT, BACK, FAR, Y1, Y2, Y3 = range(8)
SEEN_AS = {SIB: SIB, FRONT: BACK, BACK: FRONT, FAR: FAR, Y1: Y3, Y2: Y2, Y3: Y1}


def nt(a, b):
    return lax.dot_general(a, b, (((1,), (1,)), ((), ())), preferred_element_type=F32)


def tn(a, b):
    return lax.dot_general(a, b, (((0,), (0,)), ((), ())), preferred_element_type=F32)


def kernel(
    n_row, n_col, n_z,
    q_hbm, p_hbm, pos_hbm, bm_hbm, ro_hbm,
    loss_ref, gq_ref, gp_ref, p_own, q_tail, m_tail,
    q, pall, qr, pos, bm, ro, vis, ebuf, wbuf, mrow, run_m, run_l, lt, psc, meta_out, meta_in, zin, xin,
    loc_s, p_ss, p_rs, q_ss, q_rs, m_ss, m_rs, z_ss, z_rs, x_ss, x_rs, y_in, z_in,
):
    nq, width = q.shape
    np_ = pall.shape[1]
    blocks = np_ // BLK
    scale = width ** (-0.5)
    hq, hp = nq // 2, np_ // 2
    r, c = lax.axis_index("row"), lax.axis_index("col")
    odd = lax.rem(r, 2)
    s = 1 - 2 * odd

    def at_row(o):
        return {"row": lax.rem(r + o + n_row, n_row), "col": c}

    def at_col(o):
        return {"row": r, "col": lax.rem(c + o + n_col, n_col)}

    where = {
        SIB: at_row(s), FRONT: at_row(2 * s), BACK: at_row(-2 * s), FAR: at_row(-s),
        Y1: at_col(-1), Y2: at_col(-2), Y3: at_col(1),
    }
    z = lax.rem(lax.div(r, 2), n_z)
    side = lax.div(r, 2 * n_z)
    along_z = {i: {"row": side * 2 * n_z + 2 * lax.rem(z + i, n_z) + odd, "col": c} for i in range(1, n_z)}
    over_x = (1 - side) * 2 * n_z + 2 * z
    same_z = {1: where[SIB], 2: {"row": over_x + odd, "col": c}, 3: {"row": over_x + 1 - odd, "col": c}}

    barrier = pltpu.get_barrier_semaphore()
    chip = r - odd
    even_core, odd_core = {"row": chip, "col": c}, {"row": chip + 1, "col": c}
    for o in range(1, n_col):
        pl.semaphore_signal(
            barrier, inc=1, device_id={"row": chip, "col": lax.rem(c + o, n_col)}, device_id_type=MESH
        )

    @pl.when(odd == 1)
    def _():
        pl.semaphore_signal(barrier, inc=1, device_id=even_core, device_id_type=MESH)

    loads = [
        pltpu.make_async_copy(src, dst, loc_s.at[i])
        for i, (src, dst) in enumerate(
            ((q_hbm, q), (p_hbm, pall.at[OWN]), (bm_hbm, bm), (ro_hbm, ro), (pos_hbm, pos))
        )
    ]

    @pl.when(odd == 0)
    def _():
        pl.semaphore_wait(barrier, 2 * (n_col - 1) + 1)
        pl.semaphore_signal(y_in, inc=1, device_id=odd_core, device_id_type=MESH)

    @pl.when(odd == 1)
    def _():
        pl.semaphore_wait(y_in, 1)

    class Sender:
        def __init__(self, ss, rs, land):
            self.ss, self.rs, self.land, self.n, self.sent = ss, rs, land, 0, []

        def __call__(self, src, slot, to, first, rows, mark):
            cp = pltpu.make_async_remote_copy(
                src_ref=src.at[pl.ds(first, rows)],
                dst_ref=self.land(slot).at[pl.ds(first, rows)],
                send_sem=self.ss.at[self.n],
                recv_sem=self.rs.at[slot, mark],
                device_id=where[to],
                device_id_type=MESH,
            )
            self.n += 1
            self.sent.append(cp)
            cp.start()
            return cp

    send_p = Sender(p_ss, p_rs, lambda k: pall.at[k])
    send_q = Sender(q_ss, q_rs, lambda k: qr.at[k - 1])

    pa0 = send_p(p_hbm, Y1, Y3, 0, hp, 0)
    pb1 = send_p(p_hbm, Y3, Y1, hp, hp, 1)
    pa1 = send_p(p_hbm, Y1, Y3, hp, hp, 1)
    pb0 = send_p(p_hbm, Y3, Y1, 0, hp, 0)
    for cp in loads:
        cp.start()
    p_sib = send_p(p_hbm, SIB, SIB, 0, np_, 0)
    q_sib = send_q(q_hbm, SIB, SIB, 0, nq, 0)

    chips = [lax.rem(chip + 2, n_row), lax.rem(chip + n_row - 2, n_row), over_x]
    chips += [to["row"] - odd for to in along_z.values()]
    for there in chips:
        pl.semaphore_signal(barrier, inc=1, device_id={"row": there + 1, "col": c}, device_id_type=MESH)

    @pl.when(odd == 1)
    def _():
        pl.semaphore_wait(barrier, 2 * len(chips))
        pl.semaphore_signal(z_in, inc=1, device_id=even_core, device_id_type=MESH)

    @pl.when(odd == 0)
    def _():
        pl.semaphore_wait(z_in, 1)

    p_front = send_p(p_hbm, BACK, FRONT, 0, np_, 0)
    p_back = send_p(p_hbm, FRONT, BACK, 0, np_, 0)
    qz = nq * 5 // 8
    q_front = [send_q(q_hbm, BACK, FRONT, 0, qz, 0)]
    q_back = [send_q(q_hbm, FRONT, BACK, 0, qz, 0)]

    for cp in loads:
        cp.wait()
    row_i = lax.broadcasted_iota(I32, (64, 1), 0)
    slot_i, block_i = lax.shift_right_logical(row_i, 3), lax.bitwise_and(row_i, 7)
    up = jnp.where(odd == 0, jnp.int32(1), jnp.int32(0))
    group = jnp.where(
        slot_i == SIB, 2 + up,
        jnp.where(slot_i == FRONT, 1 + 3 * up, jnp.where(slot_i == BACK, 4 - 3 * up, jnp.where(slot_i == FAR, 3 - up, 0))),
    )
    nb = bm.shape[0]
    wanted = jnp.where((slot_i <= FAR) & (block_i < blocks), group * blocks + block_i, -1)
    pick = jnp.where(lax.broadcasted_iota(I32, (64, nb), 1) == wanted, 1.0, 0.0).astype(BF16)
    seen = jnp.dot(pick, bm[...].astype(F32).astype(BF16), preferred_element_type=F32)
    nr = ro.shape[0]
    pick_r = jnp.where(lax.broadcasted_iota(I32, (64, nr), 1) == slot_i - Y1, 1.0, 0.0).astype(BF16)
    listed = jnp.dot(pick_r, ro[...].astype(F32).astype(BF16), preferred_element_type=F32)
    in_roster = jnp.where(jnp.abs(listed - block_i.astype(F32)) < 0.5, 1.0, 0.0)
    seen = jnp.where(slot_i >= Y1, in_roster, seen)
    pos_row = pos[...]
    own_block = jnp.where((slot_i == OWN) & (lax.shift_right_logical(pos_row, 7) == block_i), 1.0, 0.0)
    seen = jnp.maximum(seen, own_block)
    for k in range(8):
        vis[k] = seen[8 * k : 8 * k + 8]

    run_m[...] = jnp.full(run_m.shape, LOWEST, F32)
    run_l[...] = jnp.zeros(run_l.shape, F32)

    def forward(k):
        @pl.loop(0, 2)
        def _(h):
            cols = pl.ds(pl.multiple_of(h * hq, hq), hq)
            sc = nt(pall[k], q[cols, :]) * scale
            v = vis[k, :, cols]
            m_old = run_m[0:1, cols]
            m_new = m_old
            for b in range(blocks):
                top = jnp.max(sc[b * BLK : (b + 1) * BLK], axis=0, keepdims=True)
                m_new = jnp.maximum(m_new, jnp.where(v[b : b + 1] > 0.5, top, LOWEST))
            total = run_l[0:1, cols] * jnp.exp(m_old - m_new)
            for b in range(blocks):
                bias = jnp.where(v[b : b + 1] > 0.5, -m_new, LOWEST)
                e = jnp.exp(sc[b * BLK : (b + 1) * BLK] + bias)
                total = total + jnp.sum(e, axis=0, keepdims=True)
                ebuf[k, b * BLK : (b + 1) * BLK, cols] = e
            if k == OWN:
                target = lax.broadcasted_iota(I32, (np_, hq), 0) == pos[0:1, cols]
                psc[0:1, cols] = jnp.sum(jnp.where(target, sc, 0.0), axis=0, keepdims=True)
            run_m[0:1, cols] = m_new
            run_l[0:1, cols] = total
            mrow[k, 0:1, cols] = m_new

    p_own[...] = pall[OWN]
    forward(OWN)
    p_sib.wait_recv()
    forward(SIB)
    pa0.wait_recv()
    ra = send_p(pall.at[Y1], Y2, Y3, 0, hp, 0)
    pb1.wait_recv()
    rb = send_p(pall.at[Y3], Y2, Y1, hp, hp, 1)
    pa1.wait_recv()
    pb0.wait_recv()
    q0 = nq * 7 // 16
    qa = [send_q(q_hbm, Y1, Y3, 0, q0, 0), send_q(q_hbm, Y1, Y3, q0, hq - q0, 1)]
    qb = [send_q(q_hbm, Y3, Y1, nq - q0, q0, 0), send_q(q_hbm, Y3, Y1, hq, hq - q0, 1)]
    forward(Y1)
    forward(Y3)
    p_back.wait_recv()
    p_far = send_p(pall.at[FRONT], FAR, SIB, 0, np_, 0)
    p_front.wait_recv()
    forward(FRONT)
    forward(BACK)
    p_far.wait_recv()
    forward(FAR)
    ra.wait_recv()
    rb.wait_recv()
    forward(Y2)

    lt[0:1] = run_m[0:1] + jnp.log(run_l[0:1])
    own_loss = jnp.sum(lt[0:1] - psc[0:1], axis=1, keepdims=True)
    metas = {}
    for k in (Y1, Y3, Y2, FRONT, BACK, FAR, SIB):
        rows = jnp.where(vis[k] > 0.5, -lt[0:1], LOWEST)
        last = lax.broadcasted_iota(I32, rows.shape, 0) == 7
        meta_out[k] = jnp.where(last, own_loss, rows)
        seen_as = SEEN_AS[k]
        cp = pltpu.make_async_remote_copy(
            src_ref=meta_out.at[k], dst_ref=meta_in.at[seen_as],
            send_sem=m_ss.at[k], recv_sem=m_rs.at[seen_as],
            device_id=where[k], device_id_type=MESH,
        )
        cp.start()
        metas[seen_as] = cp
    q_front.append(send_q(q_hbm, BACK, FRONT, qz, nq - qz, 1))
    q_back.append(send_q(q_hbm, FRONT, BACK, qz, nq - qz, 1))
    qa.append(send_q(q_hbm, Y1, Y3, hq, hq, 2))
    qb.append(send_q(q_hbm, Y3, Y1, 0, hq, 2))

    for k in range(8):
        @pl.loop(0, 2)
        def _(h):
            cols = pl.ds(pl.multiple_of(h * hq, hq), hq)
            factor = jnp.exp(mrow[k, 0:1, cols] - lt[0:1, cols])
            w = ebuf[k, :, cols] * factor
            if k == OWN:
                target = lax.broadcasted_iota(I32, (np_, hq), 0) == pos[0:1, cols]
                w = w - jnp.where(target, 1.0, 0.0)
            wbuf[k * np_ : (k + 1) * np_, cols] = w.astype(BF16)

    gp_ref[...] = jnp.dot(wbuf[0:np_, :], q[...], preferred_element_type=F32) * scale

    def own_gradient(first):
        cols = pl.ds(first, hq)
        total = tn(wbuf[0:np_, cols], pall[0])
        for k in range(1, 8):
            total = total + tn(wbuf[k * np_ : (k + 1) * np_, cols], pall[k])
        gq_ref[cols, :] = total * scale

    own_gradient(0)

    def backward(k, first, rows):
        span = pl.ds(first, rows)
        sc = nt(pall[OWN], qr[k - 1, span, :]) * scale
        parts = []
        for b in range(blocks):
            parts.append(jnp.exp(sc[b * BLK : (b + 1) * BLK] + meta_in[k, b : b + 1, span]).astype(BF16))
        w = jnp.concatenate(parts, axis=0)
        gp_ref[...] += jnp.dot(w, qr[k - 1, span, :], preferred_element_type=F32) * scale

    loss_at = lambda k: meta_in[k, 7:8, 0:128]
    for k in (Y1, Y3, Y2):
        metas[k].wait_recv()
    near = loss_at(Y1) + loss_at(Y3)
    mine = meta_out[Y1, 7:8, 0:128] + loss_at(Y2)
    zin[0] = jnp.broadcast_to(near + mine, (8, 128))

    def spread(buf, ss, rs, partners):
        copies = []
        for i, to in partners.items():
            cp = pltpu.make_async_remote_copy(
                src_ref=buf.at[0], dst_ref=buf.at[i], send_sem=ss.at[i], recv_sem=rs.at[i],
                device_id=to, device_id_type=MESH,
            )
            cp.start()
            copies.append(cp)
        return copies

    loss_z = spread(zin, z_ss, z_rs, along_z)

    qa[0].wait_recv()
    ra2 = [send_q(qr.at[Y1 - 1], Y2, Y3, 0, q0, 0)]
    qb[0].wait_recv()
    rb2 = [send_q(qr.at[Y3 - 1], Y2, Y1, nq - q0, q0, 2)]
    own_gradient(hq)
    qa[1].wait_recv()
    ra2.append(send_q(qr.at[Y1 - 1], Y2, Y3, q0, hq - q0, 1))
    qb[1].wait_recv()
    rb2.append(send_q(qr.at[Y3 - 1], Y2, Y1, hq, hq - q0, 3))
    metas[SIB].wait_recv()
    q_sib.wait_recv()
    backward(SIB, 0, hq)
    backward(SIB, hq, hq)
    backward(Y1, 0, hq)
    backward(Y3, hq, hq)
    q_back[0].wait_recv()
    q_far = [send_q(qr.at[FRONT - 1], FAR, SIB, 0, qz, 0)]
    metas[FRONT].wait_recv()
    backward(FRONT, 0, hq)
    metas[BACK].wait_recv()
    q_front[0].wait_recv()
    backward(BACK, 0, hq)
    metas[FAR].wait_recv()
    q_far[0].wait_recv()
    backward(FAR, 0, hq)
    for cp in loss_z:
        cp.wait_recv()
    total = zin[z]
    for i in range(1, n_z):
        total = total + zin[lax.rem(z + n_z - i, n_z)]
    xin[0] = total
    loss_x = spread(xin, x_ss, x_rs, same_z)
    q_back[1].wait_recv()
    q_far.append(send_q(qr.at[FRONT - 1], FAR, SIB, qz, nq - qz, 1))
    backward(FRONT, hq, hq)
    q_front[1].wait_recv()
    backward(BACK, hq, hq)
    qa[2].wait_recv()
    backward(Y1, hq, hq)
    qb[2].wait_recv()
    backward(Y3, 0, hq)
    q_far[1].wait_recv()
    backward(FAR, hq, hq)
    for cp in loss_x:
        cp.wait_recv()
    loss_ref[...] = ((xin[0] + xin[1]) + (xin[2] + xin[3])) * (1.0 / (nq * n_row * n_col))
    m_tail[...] = meta_in[Y2, :, q0 : nq - q0]
    ra2[0].wait_recv()
    backward(Y2, 0, q0)
    rb2[0].wait_recv()
    backward(Y2, nq - q0, q0)
    ra2[1].wait_recv()
    rb2[1].wait_recv()
    q_tail[...] = qr[Y2 - 1, q0 : nq - q0, :]

    for cp in send_p.sent + send_q.sent + list(metas.values()) + loss_z + loss_x:
        cp.wait_send()


def finish(loss, gq, gp, p_own, q_tail, m_tail, loss_out, gq_out, gp_out, gp_sum, sems):
    copies = [
        pltpu.make_async_copy(gq, gq_out, sems.at[0]),
        pltpu.make_async_copy(loss.at[pl.ds(0, 1)], loss_out, sems.at[1]),
    ]
    for cp in copies:
        cp.start()
    scale = gq.shape[1] ** (-0.5)
    for b in range(gp.shape[0] // BLK):
        rows = pl.ds(b * BLK, BLK)
        w = jnp.exp(nt(p_own[rows, :], q_tail[...]) * scale + m_tail[b : b + 1, :]).astype(BF16)
        gp_sum[rows, :] = gp[rows, :] + jnp.dot(w, q_tail[...], preferred_element_type=F32) * scale
        copies.append(pltpu.make_async_copy(gp_sum.at[rows], gp_out.at[rows], sems.at[2 + b]))
        copies[-1].start()
    for cp in copies:
        cp.wait()


def local(n_row, n_col, queries, passages, positive, block_mask, roster):
    nq, width = queries.shape
    np_ = passages.shape[0]
    n_z = n_row // 4
    nb, nr = block_mask.shape[1], roster.shape[1]
    anywhere = pl.BlockSpec(memory_space=pltpu.HBM)
    inside = pl.BlockSpec(memory_space=pltpu.VMEM)
    dma = pltpu.SemaphoreType.DMA
    operands = (queries, passages, positive.reshape(1, nq), block_mask.T, roster.T)
    loss, gq, *rest = pl.pallas_call(
        functools.partial(kernel, n_row, n_col, n_z),
        out_shape=(
            jax.ShapeDtypeStruct((8, 128), F32),
            jax.ShapeDtypeStruct((nq, width), F32),
            jax.ShapeDtypeStruct((np_, width), F32),
            jax.ShapeDtypeStruct((np_, width), BF16),
            jax.ShapeDtypeStruct((nq // 8, width), BF16),
            jax.ShapeDtypeStruct((8, nq // 8), F32),
        ),
        in_specs=[anywhere] * 5,
        out_specs=(inside,) * 6,
        scratch_shapes=[
            pltpu.VMEM((nq, width), BF16),
            pltpu.VMEM((8, np_, width), BF16),
            pltpu.VMEM((7, nq, width), BF16),
            pltpu.VMEM((1, nq), I32),
            pltpu.VMEM((nb, nq), I32),
            pltpu.VMEM((nr, nq), I32),
            pltpu.VMEM((8, 8, nq), F32),
            pltpu.VMEM((8, np_, nq), F32),
            pltpu.VMEM((8 * np_, nq), BF16),
            pltpu.VMEM((8, 8, nq), F32),
            pltpu.VMEM((8, nq), F32),
            pltpu.VMEM((8, nq), F32),
            pltpu.VMEM((8, nq), F32),
            pltpu.VMEM((8, nq), F32),
            pltpu.VMEM((8, 8, nq), F32),
            pltpu.VMEM((8, 8, nq), F32),
            pltpu.VMEM((n_z, 8, 128), F32),
            pltpu.VMEM((4, 8, 128), F32),
            dma((5,)),
            dma((10,)),
            dma((8, 2)),
            dma((17,)),
            dma((8, 4)),
            dma((8,)),
            dma((8,)),
            dma((n_z,)),
            dma((n_z,)),
            dma((4,)),
            dma((4,)),
            pltpu.SemaphoreType.REGULAR,
            pltpu.SemaphoreType.REGULAR,
        ],
        compiler_params=pltpu.CompilerParams(
            collective_id=0, has_side_effects=True, vmem_limit_bytes=48 * 2**20
        ),
        cost_estimate=pl.CostEstimate(flops=10**10, bytes_accessed=10**7, transcendentals=4 * 10**6),
    )(*(pltpu.with_memory_space_constraint(a, pltpu.HBM) for a in operands))
    a, b, d = pl.pallas_call(
        finish,
        out_shape=(
            jax.ShapeDtypeStruct((1, 128), F32),
            jax.ShapeDtypeStruct((nq, width), F32),
            jax.ShapeDtypeStruct((np_, width), F32),
        ),
        in_specs=[inside] * 6,
        out_specs=(anywhere, anywhere, anywhere),
        scratch_shapes=[pltpu.VMEM((np_, width), F32), dma((2 + np_ // BLK,))],
        compiler_params=pltpu.CompilerParams(vmem_limit_bytes=8 * 2**20),
    )(loss, gq, *rest)
    return a[0, 0:1], b, d


def solution(mesh):
    whole = P(("rep", "row", "col"), None)
    return jax.shard_map(
        functools.partial(local, mesh.shape["row"], mesh.shape["col"]),
        mesh=mesh,
        in_specs=(whole, whole, P(("rep", "row", "col")), whole, whole),
        out_specs=(P("rep"), whole, whole),
        check_vma=False,
    )
```
